32 devices in a mesh: fsdp: 8 (over y, x, core), loop: 4 (over z).
Axes of the slice: x: 2, y: 2, z: 4, core: 2. Of those that a mesh axis runs over, the one named last changes fastest.
Arguments:
- iterate: bfloat16 [4, 7168, 2048], P(None, 'fsdp', 'loop'), may hold values from -0.0625 to 0.0625
- expert_order: int32 [4], replicated, may hold values from 0 to 3, each once
Outputs:
- update: bfloat16 [4, 7168, 2048], P(None, 'fsdp', 'loop')
The draws below stay inside these ranges and needn't reach their ends.
Inputs may be any that keep to these rules, and one draw needn't show every extreme that they name: `expert_order`: each value names a different expert.
All inputs are finite; a program needn't handle non-finite values.
Results may differ from the reference program's by a relative error of at most 0.006.
Values may be sent and summed in bfloat16 or wider, within the bound.
No kernel may reach another device: no remote copies, remote signals or barrier semaphores. Data moves between devices by JAX's collectives and lax.ppermute only.
A program may use at most 128 MiB of HBM per device.

```python
import jax
import jax.numpy as jnp
from jax import lax

D = 7168
FF = 2048
EXPERTS = 4


def block_scale(own_key, dims, shards, smallest, top_value):
    factor_of, own = 1.0, jax.random.fold_in(own_key, 6)
    for position, blocks in shards:
        steps = jnp.exp(jax.random.uniform(jax.random.fold_in(own, position), (blocks,), jnp.float32, smallest / len(shards), top_value / len(shards)))
        factor_of = factor_of * jnp.repeat(steps, dims[position] // blocks).reshape([-1 if axis == position else 1 for axis in range(len(dims))])
    return factor_of


def gaussian(own_key, shape, deviation, reach, split=(), dtype=jnp.bfloat16):
    values = deviation * jax.random.normal(own_key, shape, jnp.float32)
    if split:
        values = values * block_scale(own_key, shape, split, -0.22, 0.18)
    return jnp.clip(values, -reach, reach).astype(dtype)


def setup_inputs(seed: int = 0) -> dict:
    seeds = jax.random.split(jax.random.key(seed), 3)
    return {
        "iterate": gaussian(seeds[0], (EXPERTS, D, FF), D ** -0.5, 0.0625, ((1, 8), (2, 4))),
        "expert_order": jax.random.permutation(seeds[1], EXPERTS).astype(jnp.int32),
    }


coef_linear = 3.4445
coef_cubic = -4.7750


def reference(iterate, expert_order):
    factor = 0.2 * (D ** 0.5)

    def one_slot(which):
        matrix = lax.dynamic_index_in_dim(iterate, which.astype(jnp.int32), 0, keepdims=False)
        gram = jnp.dot(matrix.T, matrix, preferred_element_type=jnp.float32)
        gram_rounded = gram.astype(jnp.bfloat16)
        product = jnp.dot(matrix, gram_rounded, preferred_element_type=jnp.float32)
        result = factor * (coef_linear * matrix.astype(jnp.float32) + coef_cubic * product)
        return result.astype(jnp.bfloat16)

    return lax.map(one_slot, expert_order)
```

```python
import jax
import jax.numpy as jnp
from jax import lax
from jax.sharding import PartitionSpec as P

D = 7168

coef_linear = 3.4445
coef_cubic = -4.775


def all_pairs(count):
    if count == 4:
        return [[1, 0, 3, 2], [2, 3, 0, 1], [3, 2, 1, 0]]
    return [[(place + step) % count for place in range(count)] for step in range(1, count)]


def swap(value, axis, bit, count):
    return lax.ppermute(value, axis, [(i, i ^ bit) for i in range(count)])


def halves(value, side):
    rows = value.shape[0] // 2
    low, high = value[:rows], value[rows:]
    return jnp.where(side == 0, low, high), jnp.where(side == 0, high, low)


def reduce_rows(partial, axis, bits, count):
    me = lax.axis_index(axis)
    for bit in bits:
        side = (me // bit) % 2
        keep, send = halves(partial, side)
        partial = keep.astype(jnp.float32) + swap(send.astype(jnp.bfloat16), axis, bit, count).astype(jnp.float32)
    return partial


def gather_rows(piece, axis, bits, count):
    me = lax.axis_index(axis)
    for bit in reversed(bits):
        side = (me // bit) % 2
        other = swap(piece, axis, bit, count)
        piece = jnp.where(side == 0, jnp.concatenate([piece, other]), jnp.concatenate([other, piece]))
    return piece


def reduce_all(partial, axis, count):
    bits = [1 << i for i in range(count.bit_length() - 1)]
    orders = [bits, bits[:1] + bits[:0:-1]]
    width = partial.shape[1] // 2
    parts = []
    for part, order in enumerate(orders):
        piece = reduce_rows(partial[:, part * width : (part + 1) * width], axis, order, count)
        parts.append(gather_rows(piece.astype(jnp.bfloat16), axis, order, count))
    return jnp.concatenate(parts, axis=1)


def body(iterate, expert_order, fsdp, loop):
    place = lax.axis_index("loop")
    tables = all_pairs(loop)
    width = iterate.shape[2]

    def mine(slot):
        return lax.dynamic_index_in_dim(iterate, expert_order[slot], 0, keepdims=False)

    targets = [jnp.asarray(table, jnp.int32)[place] for table in tables]
    blocks = [mine(place)]
    for table, target in zip(tables, targets):
        blocks.append(lax.ppermute(mine(target), "loop", list(enumerate(table))))
    matrix = jnp.concatenate(blocks, axis=1)

    slabs = []
    for a in range(loop):
        slabs.append(
            lax.dot_general(
                blocks[a], matrix[:, a * width :], (((0,), (0,)), ((), ())), preferred_element_type=jnp.float32
            )
        )
    packed = reduce_all(jnp.concatenate(slabs, axis=1), "fsdp", fsdp)
    rows = []
    start = [0]
    for a in range(loop):
        start.append(start[-1] + (loop - a) * width)
    for a in range(loop):
        left = [packed[:, start[b] + (a - b) * width : start[b] + (a - b + 1) * width].T for b in range(a)]
        rows.append(jnp.concatenate(left + [packed[:, start[a] : start[a + 1]]], axis=1))
    gram = jnp.concatenate(rows, axis=0)

    factor = 0.2 * D**0.5
    product = jnp.dot(matrix, gram, preferred_element_type=jnp.float32)
    update = (factor * (coef_linear * matrix.astype(jnp.float32) + coef_cubic * product)).astype(jnp.bfloat16)

    out = jnp.zeros_like(iterate)
    out = lax.dynamic_update_index_in_dim(out, update[:, :width], place, 0)
    for index, (table, target) in enumerate(zip(tables, targets), 1):
        back = [(to, source) for source, to in enumerate(table)]
        piece = lax.ppermute(update[:, index * width : (index + 1) * width], "loop", back)
        out = lax.dynamic_update_index_in_dim(out, piece, target, 0)
    return out


def solution(mesh):
    fsdp, loop = mesh.shape["fsdp"], mesh.shape["loop"]
    placed = (P(None, "fsdp", "loop"), P())

    def step(iterate, expert_order):
        return body(iterate, expert_order, fsdp, loop)

    return jax.shard_map(
        step, mesh=mesh, in_specs=placed, out_specs=P(None, "fsdp", "loop"), check_vma=False
    )
```

```python
import functools

import jax
import jax.numpy as jnp
from jax import lax
from jax.experimental import pallas as pl
from jax.experimental.pallas import tpu as pltpu
from jax.sharding import PartitionSpec as P

D = 7168

coef_linear = 3.4445
coef_cubic = -4.775

VMEM_LIMIT = 56 * 2**20
F32, BF16 = jnp.float32, jnp.bfloat16
ANY = pl.BlockSpec(memory_space=pl.ANY)
SMEM = pl.BlockSpec(memory_space=pltpu.SMEM)
VMEM = pl.BlockSpec(memory_space=pltpu.VMEM)


def plan(loop):
    if loop == 4:
        phases = [[[(1, 2), (2, 1)], [(0, 1), (3, 2)]], [[(0, 2), (3, 1)]]]
        return [({1: 1, 2: 2}, phases), ({1: 0, 2: 3}, phases)]
    rounds = [[(p, (p + step) % loop) for p in range(loop)] for step in range(1, loop)]
    return [({p: p for p in range(loop)}, [rounds])]


def merge(tables):
    merged, index = [], []
    for table in tables:
        for i, other in enumerate(merged):
            if all(other.get(key, value) == value for key, value in table.items()):
                other.update(table)
                index.append(i)
                break
        else:
            merged.append(dict(table))
            index.append(len(merged) - 1)
    return merged, index


def lookup(table, place):
    items = sorted(table.items())
    value = jnp.int32(items[0][1])
    for key, entry in items[1:]:
        value = jnp.where(place == key, jnp.int32(entry), value)
    return value


def params():
    return pltpu.CompilerParams(vmem_limit_bytes=VMEM_LIMIT)


def struct(shape, dtype):
    return jax.ShapeDtypeStruct(shape, dtype)


def run_copies(copies):
    for copy in copies:
        copy.start()
    for copy in copies:
        copy.wait()


def pick(iterate, expert_order, tables, deps):
    def kernel(order, source, *rest):
        outs, sems = rest[len(deps) : -1], rest[-1]
        place = lax.axis_index("loop")
        run_copies(
            [
                pltpu.make_async_copy(source.at[order[lookup(table, place)]], out, sems.at[i])
                for i, (table, out) in enumerate(zip(tables, outs))
            ]
        )

    return pl.pallas_call(
        kernel,
        out_shape=[struct(iterate.shape[1:], iterate.dtype)] * len(tables),
        in_specs=[SMEM, ANY] + [ANY] * len(deps),
        out_specs=[ANY] * len(tables),
        scratch_shapes=[pltpu.SemaphoreType.DMA((len(tables),))],
        compiler_params=params(),
        name="pick",
    )(expert_order, iterate, *deps)


def gram_part(blocks, pairs):
    rows, width = blocks[0].shape
    half = width // 2
    count = len(blocks)

    def kernel(*refs):
        xs, keep, send = refs[:count], refs[count], refs[count + 1]
        side = lax.rem(lax.axis_index("fsdp"), 2)
        for out, part in ((send, 1 - side), (keep, side)):
            at = pl.multiple_of(part * half, half)
            for a in sorted({a for a, _ in pairs}):
                left = xs[a][:, pl.ds(at, half)].T
                for index, (first, b) in enumerate(pairs):
                    if first == a:
                        out[:, index * width : (index + 1) * width] = jnp.dot(
                            left, xs[b][...], preferred_element_type=F32
                        ).astype(out.dtype)

    shape = (half, len(pairs) * width)
    return pl.pallas_call(
        kernel,
        out_shape=[struct(shape, F32), struct(shape, BF16)],
        in_specs=[VMEM] * count,
        out_specs=[VMEM] * 2,
        compiler_params=params(),
        cost_estimate=pl.CostEstimate(
            flops=2 * rows * width * width * len(pairs), bytes_accessed=8 * 2**20, transcendentals=0
        ),
        name="gram_part",
    )(*blocks)


def add_split(keeps, received, bits, split):
    count = len(keeps)

    def kernel(*refs):
        ins, news, outs = refs[:count], refs[count : 2 * count], refs[2 * count :]
        me = lax.axis_index("fsdp")
        for i, bit in enumerate(bits):
            if not split:
                outs[i][...] = (ins[i][...] + news[i][...].astype(F32)).astype(BF16)
                continue
            half = ins[i].shape[0] // 2
            side = lax.rem(lax.div(me, bit), 2)
            for out, part in ((outs[count + i], 1 - side), (outs[i], side)):
                at = pl.ds(pl.multiple_of(part * half, half), half)
                out[...] = (ins[i][at, :] + news[i][at, :].astype(F32)).astype(out.dtype)

    if split:
        shapes = [(k.shape[0] // 2, k.shape[1]) for k in keeps]
        outs = [struct(s, F32) for s in shapes] + [struct(s, BF16) for s in shapes]
    else:
        outs = [struct(k.shape, BF16) for k in keeps]
    result = pl.pallas_call(
        kernel,
        out_shape=outs,
        in_specs=[VMEM] * (2 * count),
        out_specs=[VMEM] * len(outs),
        compiler_params=params(),
        name="add_split",
    )(*keeps, *received)
    return result[:count], result[count:]


def first_split(keep, received, bits):
    rows, columns = keep.shape
    half, width = rows // 2, columns // 2

    def kernel(kept, new, *outs):
        me = lax.axis_index("fsdp")
        for i, bit in enumerate(bits):
            side = lax.rem(lax.div(me, bit), 2)
            cols = slice(i * width, (i + 1) * width)
            for out, part in ((outs[2 + i], 1 - side), (outs[i], side)):
                at = pl.ds(pl.multiple_of(part * half, half), half)
                out[...] = (kept[at, cols] + new[at, cols].astype(F32)).astype(out.dtype)

    result = pl.pallas_call(
        kernel,
        out_shape=[struct((half, width), F32)] * 2 + [struct((half, width), BF16)] * 2,
        in_specs=[VMEM] * 2,
        out_specs=[VMEM] * 4,
        compiler_params=params(),
        name="first_split",
    )(keep, received)
    return result[:2], result[2:]


def join(pieces, orders, rows, columns):
    flat = [(part, mask, piece) for part, group in enumerate(pieces) for mask, piece in group]
    width = columns // 2

    def kernel(*refs):
        ins, out, sems = refs[: len(flat)], refs[-2], refs[-1]
        me = lax.axis_index("fsdp")
        copies = []
        for index, (part, mask, piece) in enumerate(flat):
            height, at = rows, jnp.int32(0)
            for bit in orders[part]:
                height //= 2
                side = lax.rem(lax.div(me, bit), 2)
                at = at + height * ((1 - side) if mask & bit else side)
            where = pl.ds(pl.multiple_of(at, height), height)
            copies.append(
                pltpu.make_async_copy(
                    ins[index], out.at[where, part * width : (part + 1) * width], sems.at[index]
                )
            )
        run_copies(copies)

    return pl.pallas_call(
        kernel,
        out_shape=struct((rows, columns), BF16),
        in_specs=[ANY] * len(flat),
        out_specs=ANY,
        scratch_shapes=[pltpu.SemaphoreType.DMA((len(flat),))],
        compiler_params=params(),
        name="join",
    )(*[piece for _, _, piece in flat])


def swap(value, bit, fsdp, places, loop):
    pairs = [(i * loop + p, (i ^ bit) * loop + p) for i in range(fsdp) for p in places]
    return lax.ppermute(value, ("fsdp", "loop"), pairs)


def reduce_gram(keep, send, fsdp, places, loop):
    rows, columns = keep.shape
    move = functools.partial(swap, fsdp=fsdp, places=places, loop=loop)
    bits = [1 << i for i in range(1, fsdp.bit_length() - 1)]
    orders = [bits, bits[::-1]]
    keeps, sends = first_split(keep, move(send, 1), [order[0] for order in orders])
    for step in range(1, len(bits) + 1):
        received = [move(value, order[step - 1]) for value, order in zip(sends, orders)]
        last = step == len(bits)
        keeps, sends = add_split(
            keeps, received, [order[0 if last else step] for order in orders], not last
        )
    pieces = []
    for value, order in zip(keeps, orders):
        group = [(0, value)]
        for bit in reversed(order):
            group = group + [(mask | bit, move(piece, bit)) for mask, piece in group]
        pieces.append(group)
    own = join(pieces, orders, rows, columns)
    return own, move(own, 1)


def update_blocks(blocks, groups, strips):
    rows, width = blocks[0].shape
    half, count = width // 2, len(blocks)
    total = count * width
    factor = 0.2 * D**0.5

    def kernel(*refs):
        xs, refs = refs[:count], refs[count:]
        gs, refs = refs[: 2 * len(groups)], refs[2 * len(groups) :]
        outs, (x, g, sems) = refs[:count], refs[count:]
        side = lax.rem(lax.axis_index("fsdp"), 2)
        copies = [
            pltpu.make_async_copy(xs[a], x.at[:, a * width : (a + 1) * width], sems.at[a])
            for a in range(count)
        ]
        for which, pairs in enumerate(groups):
            for index, (a, b) in enumerate(pairs):
                for other in range(2):
                    part = (1 - side) if other else side
                    where = pl.ds(pl.multiple_of(a * width + part * half, half), half)
                    copies.append(
                        pltpu.make_async_copy(
                            gs[2 * which + other].at[:, index * width : (index + 1) * width],
                            g.at[where, b * width : (b + 1) * width],
                            sems.at[len(copies)],
                        )
                    )
        run_copies(copies)
        for b in range(count):
            low, high = b * width, (b + 1) * width
            product = jnp.dot(x[:, :high], g[:high, low:high], preferred_element_type=F32)
            if b < count - 1:
                product += lax.dot_general(
                    x[:, high:], g[low:high, high:], (((1,), (1,)), ((), ())), preferred_element_type=F32
                )
            outs[b][...] = (
                factor * (coef_linear * x[:, low:high].astype(F32) + coef_cubic * product)
            ).astype(BF16)

    copies = count + 2 * sum(len(pairs) for pairs in groups)
    return pl.pallas_call(
        kernel,
        out_shape=[struct((rows, width), BF16)] * count,
        in_specs=[ANY] * (count + 2 * len(groups)),
        out_specs=[VMEM] * count,
        scratch_shapes=[
            pltpu.VMEM((rows, total), BF16),
            pltpu.VMEM((total, total), BF16),
            pltpu.SemaphoreType.DMA((copies,)),
        ],
        compiler_params=params(),
        cost_estimate=pl.CostEstimate(flops=2 * rows * total * total, bytes_accessed=16 * 2**20, transcendentals=0),
        name="update",
    )(*blocks, *[half for strip in strips for half in strip])


def place_slots(candidates, slots, like):
    flat = [value for wave in candidates for value in wave]

    def kernel(*refs):
        ins, out, sems = refs[: len(flat)], refs[-2], refs[-1]
        place = lax.axis_index("loop")
        for wave, tables in enumerate(slots):
            base = sum(len(candidates[w]) for w in range(wave))
            for index, table in enumerate(tables):
                for key, slot in table.items():

                    @pl.when(place == key)
                    def _(index=index, slot=slot, base=base):
                        pltpu.make_async_copy(ins[base + index], out.at[slot], sems.at[slot]).start()

        for slot in range(like.shape[0]):
            pltpu.make_async_copy(ins[0], out.at[slot], sems.at[slot]).wait()

    return pl.pallas_call(
        kernel,
        out_shape=struct(like.shape, like.dtype),
        in_specs=[ANY] * len(flat),
        out_specs=ANY,
        scratch_shapes=[pltpu.SemaphoreType.DMA((like.shape[0],))],
        compiler_params=params(),
        name="place_slots",
    )(*flat)


def body(iterate, expert_order, fsdp, loop):
    count = loop
    pairs = [(a, b) for a in range(count) for b in range(a, count)]
    groups = [pairs]
    waves = plan(loop)

    arrived, token = [], []
    for owners, phases in waves:
        blocks = []
        for rounds in phases:
            tables = [{source: owners[owner] for source, owner in step} for step in rounds]
            merged, index = merge(tables if blocks else tables + [owners])
            picked = pick(iterate, expert_order, merged, token)
            if not blocks:
                blocks.append(picked[index[-1]])
            token = [lax.ppermute(picked[i], "loop", step) for i, step in zip(index, rounds)]
            blocks.extend(token)
        arrived.append(blocks)

    candidates, slots = [], []
    for (owners, phases), blocks in zip(waves, arrived):
        places = sorted(owners)
        strips = []
        for group in groups:
            keep, send = gram_part(blocks, group)
            strips.append(reduce_gram(keep, send, fsdp, places, loop))
        updates = update_blocks(blocks, groups, strips)
        found, tables = [updates[0]], [dict(owners)]
        for value, step in zip(updates[1:], [step for rounds in phases for step in rounds]):
            found.append(lax.ppermute(value, "loop", [(owner, source) for source, owner in step]))
            tables.append({source: owners[owner] for source, owner in step})
        candidates.append(found)
        slots.append(tables)
    return place_slots(candidates, slots, iterate)


def solution(mesh):
    fsdp, loop = mesh.shape["fsdp"], mesh.shape["loop"]
    placed = (P(None, "fsdp", "loop"), P())

    def step(iterate, expert_order):
        return body(iterate, expert_order, fsdp, loop)

    return jax.shard_map(
        step, mesh=mesh, in_specs=placed, out_specs=P(None, "fsdp", "loop"), check_vma=False
    )
```

```python
import jax
import jax.numpy as jnp
from jax import lax
from jax.experimental import pallas as pl
from jax.experimental.pallas import tpu as pltpu
from jax.sharding import PartitionSpec as P

D = 7168

coef_linear = 3.4445
coef_cubic = -4.775

MIB = 2**20
F32, BF16 = jnp.float32, jnp.bfloat16
ANY = pl.BlockSpec(memory_space=pl.ANY)
SMEM = pl.BlockSpec(memory_space=pltpu.SMEM)
VMEM = pl.BlockSpec(memory_space=pltpu.VMEM)


def plan(loop, fsdp):
    levels = fsdp.bit_length() - 2
    if loop == 4 and levels == 2:
        phases = [[[0, 2, 1, 3], [1, 0, 3, 2]], [[2, 0, 3, 1]]]
        order = """
            0pick0 0pick1 0gram0 0split0 0add00 1pick0 0gram1 0add01 0split1 0add10 1pick1 1gram0 0add11
            1split0 0join0 1add00 1gram1 0join1 1split1 0update31 0update20
            1add01 1add10 1add11 0need3 1join0 0need2 1join1 0need1 1update31 1update20
        """
        turns = [(int(t[0]), t[1:].rstrip("0123456789"), [int(c) for c in t[1:] if c.isdigit()]) for t in order.split()]
        return [({1: 1, 2: 2}, phases), ({1: 0, 2: 3}, phases)], turns
    rounds = [[(p + step) % loop for p in range(loop)] for step in range(1, loop)]
    turns = [(0, "pick", [0]), (0, "gram", [0]), (0, "split", [0])]
    turns += [(0, "add", [0, i]) for i in range(levels)] + [(0, "join", [i]) for i in range(levels)]
    return [({p: p for p in range(loop)}, [rounds])], turns + [(0, "update", list(range(loop)))]


def sends(owners, step):
    return {p: owners[to] for p, to in enumerate(step) if to in owners and to != p}


def merge(tables):
    merged, index = [], []
    for table in tables:
        for i, other in enumerate(merged):
            if all(other.get(key, value) == value for key, value in table.items()):
                other.update(table)
                index.append(i)
                break
        else:
            merged.append(dict(table))
            index.append(len(merged) - 1)
    return merged, index


def lookup(table, place):
    items = sorted(table.items())
    value = jnp.int32(items[0][1])
    for key, entry in items[1:]:
        value = jnp.where(place == key, jnp.int32(entry), value)
    return value


def struct(shape, dtype):
    return jax.ShapeDtypeStruct(shape, dtype)


def call(kernel, name, ins, specs, outs, mib, scratch=(), after=()):
    count, extra = len(ins), len(after)

    def wrapped(*refs):
        kernel(*refs[:count], *refs[count + extra :])

    result = pl.pallas_call(
        wrapped,
        out_shape=outs,
        in_specs=list(specs) + [ANY] * extra,
        out_specs=[VMEM] * len(outs),
        scratch_shapes=list(scratch),
        compiler_params=pltpu.CompilerParams(vmem_limit_bytes=int(mib * MIB)),
        cost_estimate=pl.CostEstimate(flops=0, bytes_accessed=1, transcendentals=0),
        name=name,
    )(*ins, *after)
    return list(result)


def run_copies(copies):
    for copy in copies:
        copy.start()
    for copy in copies:
        copy.wait()


def side_of(bit):
    return lax.rem(lax.div(lax.axis_index("fsdp"), bit), 2)


def rows_at(part, height):
    return pl.ds(pl.multiple_of(part * height, height), height)


def pick(iterate, expert_order, tables, after):
    def kernel(order, source, *rest):
        outs, sems = rest[:-1], rest[-1]
        place = lax.axis_index("loop")
        run_copies(
            [
                pltpu.make_async_copy(source.at[order[lookup(table, place)]], out, sems.at[i])
                for i, (table, out) in enumerate(zip(tables, outs))
            ]
        )

    outs = [struct(iterate.shape[1:], iterate.dtype)] * len(tables)
    sems = [pltpu.SemaphoreType.DMA((len(tables),))]
    return call(kernel, "pick", [expert_order, iterate], [SMEM, ANY], outs, 8, sems, after=after)


def gram_part(blocks, pairs, chunks, after):
    rows, width = blocks[0].shape
    half, count = width // 2, len(blocks)
    total = len(pairs) * width
    piece = total // chunks

    def kernel(*refs):
        xs, keep, sent, left = refs[:count], refs[count], refs[count + 1 : -1], refs[-1]
        side = side_of(1)
        for sending, part in ((True, 1 - side), (False, side)):
            for a in sorted({a for a, _ in pairs}):
                left[a * half : (a + 1) * half, :] = xs[a][:, rows_at(part, half)].T
            for b in sorted({b for _, b in pairs}):
                firsts = [a for a, second in pairs if second == b]
                product = jnp.dot(left[: len(firsts) * half, :], xs[b][...], preferred_element_type=F32)
                for a in firsts:
                    value = product[a * half : (a + 1) * half]
                    at = pairs.index((a, b)) * width
                    if not sending:
                        keep[:, at : at + width] = value
                        continue
                    done = 0
                    while done < width:
                        chunk, offset = divmod(at + done, piece)
                        size = min(piece - offset, width - done)
                        sent[chunk][:, offset : offset + size] = value[:, done : done + size].astype(BF16)
                        done += size

    outs = [struct((half, total), F32)] + [struct((half, piece), BF16)] * chunks
    scratch = [pltpu.VMEM((count * half, rows), BF16)]
    result = call(kernel, "gram_part", blocks, [VMEM] * count, outs, 20, scratch, after)
    return result[0], result[1:]


def first_split(keep, received, bits, after):
    rows, columns = keep.shape
    half, width = rows // 2, columns // 2
    chunks = len(received)
    piece = columns // chunks

    def kernel(kept, *refs):
        news, outs = refs[:chunks], refs[chunks:]
        for chunk, new in enumerate(news):
            i, offset = divmod(chunk * piece, width)
            side = side_of(bits[i])
            cols = slice(chunk * piece, (chunk + 1) * piece)
            for out, part in ((outs[2 + i], 1 - side), (outs[i], side)):
                at = rows_at(part, half)
                out[:, offset : offset + piece] = (kept[at, cols] + new[at, :].astype(F32)).astype(out.dtype)

    outs = [struct((half, width), F32)] * 2 + [struct((half, width), BF16)] * 2
    result = call(kernel, "first_split", [keep, *received], [VMEM] * (1 + chunks), outs, 14, after=after)
    return result[:2], result[2:]


def add_split(keeps, received, earlier, bits, after):
    count = len(keeps)
    ins_count = (2 + len(earlier)) * count
    before = sum(values[0].shape[1] for values in earlier)

    def kernel(*refs):
        ins, news, olds, outs = refs[:count], refs[count : 2 * count], refs[2 * count : ins_count], refs[ins_count:]
        for i in range(count):
            if not bits:
                done = 0
                for old in olds[i::count]:
                    outs[i][:, done : done + old.shape[1]] = old[...]
                    done += old.shape[1]
                outs[i][:, before:] = (ins[i][...] + news[i][...].astype(F32)).astype(BF16)
                continue
            half = ins[i].shape[0] // 2
            side = side_of(bits[i])
            for out, part in ((outs[count + i], 1 - side), (outs[i], side)):
                at = rows_at(part, half)
                out[...] = (ins[i][at, :] + news[i][at, :].astype(F32)).astype(out.dtype)

    if bits:
        shapes = [(k.shape[0] // 2, k.shape[1]) for k in keeps]
        outs = [struct(s, F32) for s in shapes] + [struct(s, BF16) for s in shapes]
    else:
        outs = [struct((k.shape[0], before + k.shape[1]), BF16) for k in keeps]
    ins = [*keeps, *received, *[value for values in earlier for value in values]]
    result = call(kernel, "add_split", ins, [VMEM] * ins_count, outs, 8, after=after)
    return result[:count], result[count:]


def join(values, received, bits, chunks, after):
    count = len(values)
    rows, width = values[0].shape

    def kernel(*refs):
        ins, news, outs = refs[:count], refs[count : 2 * count], refs[2 * count :]
        for i, bit in enumerate(bits):
            side = side_of(bit)
            for source, part in ((ins[i], side), (news[i], 1 - side)):
                at = rows_at(part, rows)
                if not chunks:
                    outs[i][at, :] = source[...]
                    continue
                piece = count * width // chunks
                for chunk in range(chunks):
                    low, high = max(chunk * piece, i * width), min((chunk + 1) * piece, (i + 1) * width)
                    if low < high:
                        outs[chunk][at, low - chunk * piece : high - chunk * piece] = source[
                            :, low - i * width : high - i * width
                        ]

    if chunks:
        outs = [struct((2 * rows, count * width // chunks), BF16)] * chunks
    else:
        outs = [struct((2 * rows, width), BF16)] * count
    return call(kernel, "join", [*values, *received], [VMEM] * (2 * count), outs, 8, after=after)


def swap(value, bit, fsdp):
    return lax.ppermute(value, "fsdp", [(i, i ^ bit) for i in range(fsdp)])


def update_blocks(blocks, places, own, other, wanted, after):
    rows, width = blocks[0].shape
    half, count = width // 2, len(blocks)
    total, chunks, piece = count * width, len(own), own[0].shape[1]
    factor = 0.2 * D**0.5

    def kernel(*refs):
        xs, strips = refs[:count], (refs[count : count + chunks], refs[count + chunks : count + 2 * chunks])
        refs = refs[count + 2 * chunks :]
        outs, (x, g) = refs[: len(wanted)], refs[len(wanted) :]
        side = side_of(1)
        for a in range(count):
            x[:, a * width : (a + 1) * width] = xs[a][...]
        for part, strip in zip((side, 1 - side), strips):
            for (a, b), column in places.items():
                if a not in wanted and b not in wanted:
                    continue
                where = pl.ds(pl.multiple_of(a * width + part * half, half), half)
                done = 0
                while done < width:
                    chunk, offset = divmod(column + done, piece)
                    size = min(piece - offset, width - done)
                    at = b * width + done
                    g[where, at : at + size] = strip[chunk][:, offset : offset + size]
                    done += size
        for out, b in zip(outs, wanted):
            low, high = b * width, (b + 1) * width
            product = jnp.dot(x[:, :high], g[:high, low:high], preferred_element_type=F32)
            if b < count - 1:
                product += lax.dot_general(
                    x[:, high:], g[low:high, high:], (((1,), (1,)), ((), ())), preferred_element_type=F32
                )
            out[...] = (factor * (coef_linear * x[:, low:high].astype(F32) + coef_cubic * product)).astype(BF16)

    scratch = [pltpu.VMEM((rows, total), BF16), pltpu.VMEM((total, total), BF16)]
    outs = [struct((rows, width), BF16)] * len(wanted)
    ins = [*blocks, *own, *other]
    return call(kernel, "update", ins, [VMEM] * len(ins), outs, 30, scratch, after)


def place_slots(candidates, slots, like, after):
    flat = [value for wave in candidates for value in wave]

    def kernel(*refs):
        ins, out, sems = refs[: len(flat)], refs[-2], refs[-1]
        place = lax.axis_index("loop")
        base = 0
        for wave, tables in enumerate(slots):
            for index, table in enumerate(tables):
                for key, slot in table.items():

                    @pl.when(place == key)
                    def _(source=ins[base + index], slot=slot):
                        pltpu.make_async_copy(source, out.at[slot], sems.at[slot]).start()

            base += len(tables)
        for slot in range(like.shape[0]):
            pltpu.make_async_copy(ins[0], out.at[slot], sems.at[slot]).wait()

    sems = [pltpu.SemaphoreType.DMA((like.shape[0],))]
    outs = [struct(like.shape, like.dtype)]
    return call(kernel, "place_slots", flat, [ANY] * len(flat), outs, 8, sems, after=after)[0]


class Wave:
    def __init__(self, iterate, expert_order, owners, phases, fsdp, chunks, shared):
        self.iterate, self.expert_order, self.owners, self.phases = iterate, expert_order, owners, phases
        self.fsdp, self.chunks, self.shared = fsdp, chunks, shared
        self.bits = [1 << i for i in range(1, fsdp.bit_length() - 1)]
        self.orders = [self.bits, self.bits[::-1]]
        self.blocks, self.groups, self.state, self.gathered = [], [], {}, None
        self.rounds = [step for rounds in phases for step in rounds]
        self.updates = {}

    def move(self, values, bits):
        return [swap(value, bit, self.fsdp) for value, bit in zip(values, bits)]

    def pick(self, phase):
        rounds, first = self.phases[phase], len(self.blocks)
        tables = [sends(self.owners, step) for step in rounds]
        merged, index = merge(tables if phase else tables + [self.owners])
        picked = pick(self.iterate, self.expert_order, merged, self.shared["last"] + self.shared["arrived"])
        if not phase:
            self.blocks.append(picked[index[-1]])
        arrived = [lax.ppermute(picked[i], "loop", list(enumerate(step))) for i, step in zip(index, rounds)]
        self.blocks.extend(arrived)
        count = len(self.blocks)
        self.groups.append([(a, b) for b in range(first, count) for a in range(b + 1)])
        self.shared["last"], self.shared["arrived"] = picked[:1], arrived

    def gram(self, group):
        pairs = self.groups[group]
        blocks = self.blocks[: 1 + max(b for _, b in pairs)]
        keep, out = gram_part(blocks, pairs, self.chunks, self.shared["last"])
        self.shared["last"] = [keep]
        self.state[group] = keep, self.move(out, [1] * self.chunks)

    def split(self, group):
        keep, received = self.state[group]
        firsts = [order[0] for order in self.orders]
        keeps, out = first_split(keep, received, firsts, self.shared["last"])
        self.shared["last"] = keeps[:1]
        self.state[group] = keeps, self.move(out, firsts)

    def add(self, group, level):
        keeps, received = self.state[group]
        bits = [order[level + 1] for order in self.orders if level + 1 < len(order)]
        last = not bits and group == len(self.phases) - 1
        earlier = [self.state[g] for g in range(group)] if last else []
        keeps, out = add_split(keeps, received, earlier, bits, self.shared["last"])
        self.shared["last"] = keeps[:1]
        self.state[group] = (keeps, self.move(out, bits)) if bits else keeps
        if last:
            self.gathered = keeps, self.move(keeps, [order[-1] for order in self.orders])

    def join(self, level):
        left = len(self.bits) - 1 - level
        bits = [order[left] for order in self.orders]
        values = join(*self.gathered, bits, 0 if left else self.chunks, self.shared["last"])
        self.shared["last"] = values[:1]
        bits = [order[left - 1] for order in self.orders] if left else [1] * self.chunks
        self.gathered = values, self.move(values, bits)

    def places(self):
        width, found, column = self.blocks[0].shape[1], {}, 0
        for part in range(2):
            for pairs in self.groups:
                half = len(pairs) // 2
                for pair in pairs[part * half : (part + 1) * half]:
                    found[pair] = column
                    column += width
        return found

    def update(self, *wanted):
        values = update_blocks(self.blocks, self.places(), *self.gathered, wanted, self.shared["last"])
        self.shared["last"] = values[:1]
        for b, value in zip(wanted, values):
            if b:
                back = [(to, source) for source, to in enumerate(self.rounds[b - 1])]
                value = lax.ppermute(value, "loop", back)
            self.updates[b] = value

    def need(self, b):
        self.shared["last"] = self.shared["last"] + [self.updates[b]]

    def result(self):
        tables = [self.owners] + [sends(self.owners, step) for step in self.rounds]
        return [self.updates[b] for b in range(len(tables))], tables


def body(iterate, expert_order, fsdp, loop):
    waves, turns = plan(loop, fsdp)
    shared = {"last": [], "arrived": []}
    waves = [Wave(iterate, expert_order, owners, phases, fsdp, 4, shared) for owners, phases in waves]
    for turn, step, arguments in turns:
        getattr(waves[turn], step)(*arguments)
    results = [wave.result() for wave in waves]
    return place_slots([found for found, _ in results], [tables for _, tables in results], iterate, shared["last"])


def solution(mesh):
    fsdp, loop = mesh.shape["fsdp"], mesh.shape["loop"]
    placed = (P(None, "fsdp", "loop"), P())

    def step(iterate, expert_order):
        return body(iterate, expert_order, fsdp, loop)

    return jax.shard_map(
        step, mesh=mesh, in_specs=placed, out_specs=P(None, "fsdp", "loop"), check_vma=False
    )
```

```python
import functools

import jax
import jax.numpy as jnp
from jax import lax
from jax.experimental import pallas as pl
from jax.experimental.pallas import tpu as pltpu
from jax.sharding import PartitionSpec as P

D = 7168

coef_linear = 3.4445
coef_cubic = -4.775

CHUNKS = 4, 2

MIB = 2**20
F32, BF16 = jnp.float32, jnp.bfloat16
ANY = pl.BlockSpec(memory_space=pl.ANY)
SMEM = pl.BlockSpec(memory_space=pltpu.SMEM)
VMEM = pl.BlockSpec(memory_space=pltpu.VMEM)


def plan(loop, fsdp):
    levels = fsdp.bit_length() - 2
    if loop == 4 and levels == 2:
        phases = [[[1, 0, 3, 2], [0, 2, 1, 3]], [[2, 0, 3, 1]], [[1, 3, 0, 2]], [[3, 1, 2, 0]]]
        waves = [({0: 0, 3: 3}, [[0], [3], [4]], [[0], [1, 2]]), ({1: 1, 2: 2}, [[0, 1], [2]], [[0, 1]])]
        order = [
            "0send0", "0send1", "1gram0", "1split0", "0gram0", "1add00", "0send2", "1gram1", "1add01", "1split1",
            "0split0", "1add10", "0add00", "0send3", "1add11", "0add01", "0gram1", "1join00", "0split1", "0join00",
            "0gram2", "1join01", "0add10", "0join01", "0split2", "1update32", "0add11", "0add20", "1update10",
            "0add21", "0join10", "1need3", "0join11", "0update12", "0update30", "1place203", "0place120", "1place1",
            "0place3",
        ]
        turns = [(int(t[0]), t[1:].rstrip("0123456789"), [int(c) for c in t[1:] if c.isdigit()]) for t in order]
        return phases, waves, {(0, 2): (1, 1)}, turns
    rounds = [[(p + step) % loop for p in range(loop)] for step in range(1, loop)]
    turns = [(0, "send", [0]), (0, "gram", [0]), (0, "split", [0])]
    turns += [(0, step, [0, i]) for step in ("add", "join") for i in range(levels)]
    turns += [(0, "update", list(range(loop))), (0, "place", list(range(loop)))]
    return [rounds], [({p: p for p in range(loop)}, [list(range(len(rounds)))], [[0]])], {}, turns


def sends(owners, step):
    return {p: owners[to] for p, to in enumerate(step) if to in owners and to != p}


def merge(tables):
    merged, index = [], []
    for table in tables:
        for i, other in enumerate(merged):
            if all(other.get(key, value) == value for key, value in table.items()):
                other.update(table)
                index.append(i)
                break
        else:
            merged.append(dict(table))
            index.append(len(merged) - 1)
    return merged, index


def lookup(table, place):
    items = sorted(table.items())
    value = jnp.int32(items[0][1])
    for key, entry in items[1:]:
        value = jnp.where(place == key, jnp.int32(entry), value)
    return value


def struct(shape, dtype):
    return jax.ShapeDtypeStruct(shape, dtype)


def call(kernel, name, ins, specs, outs, mib, scratch=(), after=()):
    count, extra = len(ins), len(after)

    def wrapped(*refs):
        kernel(*refs[:count], *refs[count + extra :])

    result = pl.pallas_call(
        wrapped,
        out_shape=outs,
        in_specs=list(specs) + [ANY] * extra,
        out_specs=[VMEM] * len(outs),
        scratch_shapes=list(scratch),
        compiler_params=pltpu.CompilerParams(vmem_limit_bytes=int(mib * MIB)),
        cost_estimate=pl.CostEstimate(flops=0, bytes_accessed=1, transcendentals=0),
        name=name,
    )(*ins, *after)
    return list(result)


def run_copies(copies):
    for copy in copies:
        copy.start()
    for copy in copies:
        copy.wait()


def side_of(bit):
    return lax.rem(lax.div(lax.axis_index("fsdp"), bit), 2)


def is_one_of(places):
    here = lax.axis_index("loop")
    return functools.reduce(jnp.logical_or, [here == place for place in places])


def rows_at(part, height):
    return pl.ds(pl.multiple_of(part * height, height), height)


def pick(iterate, expert_order, tables, after):
    def kernel(order, source, *rest):
        outs, sems = rest[:-1], rest[-1]
        place = lax.axis_index("loop")
        run_copies(
            [
                pltpu.make_async_copy(source.at[order[lookup(table, place)]], out, sems.at[i])
                for i, (table, out) in enumerate(zip(tables, outs))
            ]
        )

    outs = [struct(iterate.shape[1:], iterate.dtype)] * len(tables)
    sems = [pltpu.SemaphoreType.DMA((len(tables),))]
    return call(kernel, "pick", [expert_order, iterate], [SMEM, ANY], outs, 8, sems, after=after)


def gram_part(blocks, pairs, chunks, owners, after):
    rows, width = blocks[0].shape
    half, count = width // 2, len(blocks)
    total = len(pairs) * width
    piece = total // chunks

    def kernel(*refs):
        xs, keep, sent, left = refs[:count], refs[count], refs[count + 1 : -1], refs[-1]
        side = side_of(1)
        pl.when(is_one_of(owners))(lambda: multiply(xs, keep, sent, left, side))

    def multiply(xs, keep, sent, left, side):
        for sending, part in ((True, 1 - side), (False, side)):
            for a in sorted({a for a, _ in pairs}):
                left[a * half : (a + 1) * half, :] = xs[a][:, rows_at(part, half)].T
            for b in sorted({b for _, b in pairs}):
                firsts = [a for a, second in pairs if second == b]
                product = jnp.dot(left[: len(firsts) * half, :], xs[b][...], preferred_element_type=F32)
                for a in firsts:
                    value = product[a * half : (a + 1) * half]
                    at = pairs.index((a, b)) * width
                    if not sending:
                        keep[:, at : at + width] = value
                        continue
                    done = 0
                    while done < width:
                        chunk, offset = divmod(at + done, piece)
                        size = min(piece - offset, width - done)
                        sent[chunk][:, offset : offset + size] = value[:, done : done + size].astype(BF16)
                        done += size

    outs = [struct((half, total), F32)] + [struct((half, piece), BF16)] * chunks
    scratch = [pltpu.VMEM((count * half, rows), BF16)]
    result = call(kernel, "gram_part", blocks, [VMEM] * count, outs, 20, scratch, after)
    return result[0], result[1:]


def first_split(keep, received, bits, after):
    rows, columns = keep.shape
    half, width = rows // 2, columns // 2
    chunks = len(received)
    piece = columns // chunks

    def kernel(kept, *refs):
        news, outs = refs[:chunks], refs[chunks:]
        for chunk, new in enumerate(news):
            i, offset = divmod(chunk * piece, width)
            side = side_of(bits[i])
            cols = slice(chunk * piece, (chunk + 1) * piece)
            for out, part in ((outs[2 + i], 1 - side), (outs[i], side)):
                at = rows_at(part, half)
                out[:, offset : offset + piece] = (kept[at, cols] + new[at, :].astype(F32)).astype(out.dtype)

    outs = [struct((half, width), F32)] * 2 + [struct((half, width), BF16)] * 2
    result = call(kernel, "first_split", [keep, *received], [VMEM] * (1 + chunks), outs, 14, after=after)
    return result[:2], result[2:]


def add_split(keeps, received, earlier, bits, after):
    count = len(keeps)
    ins_count = (2 + len(earlier)) * count
    before = sum(values[0].shape[1] for values in earlier)

    def kernel(*refs):
        ins, news, olds, outs = refs[:count], refs[count : 2 * count], refs[2 * count : ins_count], refs[ins_count:]
        for i in range(count):
            if not bits:
                done = 0
                for old in olds[i::count]:
                    outs[i][:, done : done + old.shape[1]] = old[...]
                    done += old.shape[1]
                outs[i][:, before:] = (ins[i][...] + news[i][...].astype(F32)).astype(BF16)
                continue
            half = ins[i].shape[0] // 2
            side = side_of(bits[i])
            for out, part in ((outs[count + i], 1 - side), (outs[i], side)):
                at = rows_at(part, half)
                out[...] = (ins[i][at, :] + news[i][at, :].astype(F32)).astype(out.dtype)

    if bits:
        shapes = [(k.shape[0] // 2, k.shape[1]) for k in keeps]
        outs = [struct(s, F32) for s in shapes] + [struct(s, BF16) for s in shapes]
    else:
        outs = [struct((k.shape[0], before + k.shape[1]), BF16) for k in keeps]
    ins = [*keeps, *received, *[value for values in earlier for value in values]]
    result = call(kernel, "add_split", ins, [VMEM] * ins_count, outs, 8, after=after)
    return result[:count], result[count:]


def join(values, received, bits, chunks, after):
    count = len(values)
    rows, width = values[0].shape

    def kernel(*refs):
        ins, news, outs = refs[:count], refs[count : 2 * count], refs[2 * count :]
        for i, bit in enumerate(bits):
            side = side_of(bit)
            for source, part in ((ins[i], side), (news[i], 1 - side)):
                at = rows_at(part, rows)
                if not chunks:
                    outs[i][at, :] = source[...]
                    continue
                piece = count * width // chunks
                for chunk in range(chunks):
                    low, high = max(chunk * piece, i * width), min((chunk + 1) * piece, (i + 1) * width)
                    if low < high:
                        outs[chunk][at, low - chunk * piece : high - chunk * piece] = source[
                            :, low - i * width : high - i * width
                        ]

    if chunks:
        outs = [struct((2 * rows, count * width // chunks), BF16)] * chunks
    else:
        outs = [struct((2 * rows, width), BF16)] * count
    return call(kernel, "join", [*values, *received], [VMEM] * (2 * count), outs, 8, after=after)


def swap(value, bit, fsdp, loop, places):
    pairs = [(i * loop + p, (i ^ (bit if p in places else 1)) * loop + p) for i in range(fsdp) for p in range(loop)]
    return lax.ppermute(value, ("fsdp", "loop"), pairs)


def shift(value, step, fsdp):
    loop = len(step)
    pairs = [(i * loop + p, (i ^ (to == p)) * loop + to) for i in range(fsdp) for p, to in enumerate(step)]
    return lax.ppermute(value, ("fsdp", "loop"), pairs)


def update_blocks(blocks, places, own, other, wanted, instead, owners, after):
    rows, width = blocks[0].shape
    half, count = width // 2, len(blocks)
    total, chunks = count * width, len(own)
    factor = 0.2 * D**0.5

    def kernel(*refs):
        xs, strips = refs[:count], (refs[count : count + chunks], refs[count + chunks : count + 2 * chunks])
        refs = refs[count + 2 * chunks :]
        given, refs = refs[: len(instead)], refs[len(instead) :]
        outs, (x, g) = refs[: len(wanted)], refs[len(wanted) :]
        mine = is_one_of(owners)
        pl.when(mine)(lambda: multiply(xs, strips, outs, x, g))
        for b, value in zip(instead, given):

            @pl.when(jnp.logical_not(mine))
            def _(out=outs[wanted.index(b)], value=value):
                out[...] = value[...]

    def multiply(xs, strips, outs, x, g):
        side = side_of(1)
        for a in range(count):
            x[:, a * width : (a + 1) * width] = xs[a][...]
        for part, strip in zip((side, 1 - side), strips):
            for (a, b), pieces in places.items():
                if a not in wanted and b not in wanted:
                    continue
                where = pl.ds(pl.multiple_of(a * width + part * half, half), half)
                for chunk, offset, first, size in pieces:
                    at = b * width + first
                    g[where, at : at + size] = strip[chunk][:, offset : offset + size]
        for out, b in zip(outs, wanted):
            low, high = b * width, (b + 1) * width
            product = jnp.dot(x[:, :high], g[:high, low:high], preferred_element_type=F32)
            if b < count - 1:
                product += lax.dot_general(
                    x[:, high:], g[low:high, high:], (((1,), (1,)), ((), ())), preferred_element_type=F32
                )
            out[...] = (factor * (coef_linear * x[:, low:high].astype(F32) + coef_cubic * product)).astype(BF16)

    scratch = [pltpu.VMEM((rows, total), BF16), pltpu.VMEM((total, total), BF16)]
    outs = [struct((rows, width), BF16)] * len(wanted)
    ins = [*blocks, *own, *other, *instead.values()]
    return call(kernel, "update", ins, [VMEM] * len(ins), outs, 30, scratch, after)


def place_slots(out, found, like, after):
    old = [] if out is None else [out]
    ins = [value for value, _ in found]
    cases = [(i, place, slot) for i, (_, table) in enumerate(found) for place, slot in table.items()]

    def kernel(*refs):
        values, target, sems = refs[: len(ins)], refs[-2], refs[-1]
        here = lax.axis_index("loop")
        for wait in (False, True):
            for i, place, slot in cases:

                @pl.when(here == place)
                def _(i=i, slot=slot):
                    copy = pltpu.make_async_copy(values[i], target.at[slot], sems.at[i])
                    copy.wait() if wait else copy.start()

    return pl.pallas_call(
        kernel,
        out_shape=struct(like.shape, like.dtype),
        in_specs=[VMEM] * len(ins) + [ANY] * (len(old) + len(after)),
        out_specs=ANY,
        scratch_shapes=[pltpu.SemaphoreType.DMA((len(ins),))],
        input_output_aliases={len(ins): 0} if old else {},
        compiler_params=pltpu.CompilerParams(vmem_limit_bytes=8 * MIB),
        cost_estimate=pl.CostEstimate(flops=0, bytes_accessed=1, transcendentals=0),
        name="place_slots",
    )(*ins, *old, *after)


class Columns:
    def __init__(self, iterate, expert_order, phases, fsdp):
        self.iterate, self.expert_order, self.phases, self.fsdp = iterate, expert_order, phases, fsdp
        self.rounds = [step for rounds in phases for step in rounds]
        self.own, self.arrived, self.last, self.out = None, [], [], None

    def send(self, phase):
        rounds = self.phases[phase]
        tables = [{p: to for p, to in enumerate(step) if p != to} for step in rounds]
        places = {p: p for p in range(len(rounds[0]))}
        merged, index = merge(tables if phase else tables + [places])
        before = self.arrived[len(self.arrived) - len(self.phases[phase - 1]) :] if phase else []
        picked = pick(self.iterate, self.expert_order, merged, self.last + before)
        if not phase:
            self.own = picked[index[-1]]
        self.arrived += [shift(picked[i], step, self.fsdp) for i, step in zip(index, rounds)]
        self.last = picked[:1]


class Wave:
    def __init__(self, columns, owners, groups, gathers, shares, loop, chunks):
        self.columns, self.owners, self.loop, self.chunks = columns, owners, loop, chunks
        self.fsdp = columns.fsdp
        self.bits = [1 << i for i in range(1, self.fsdp.bit_length() - 1)]
        self.orders = [self.bits, self.bits[::-1]]
        self.rounds = [number for group in groups for number in group]
        self.groups, self.gathers, self.state, self.gathered, first = [], gathers, {}, {}, 0
        for group in groups:
            count = first + len(group) + 1
            self.groups.append([(a, b) for b in range(first + 1 if first else 0, count) for a in range(b + 1)])
            first += len(group)
        self.updates, self.shares = {}, shares

    def blocks(self, count):
        return [self.columns.own] + [self.columns.arrived[number] for number in self.rounds[: count - 1]]

    def move(self, values, bits):
        return [swap(value, bit, self.fsdp, self.loop, self.owners) for value, bit in zip(values, bits)]

    def gram(self, group):
        pairs = self.groups[group]
        blocks = self.blocks(1 + max(b for _, b in pairs))
        keep, out = gram_part(blocks, pairs, self.chunks[0], self.owners, self.columns.last)
        self.columns.last = [keep]
        self.state[group] = keep, self.move(out, [1] * self.chunks[0])

    def split(self, group):
        keep, received = self.state[group]
        firsts = [order[0] for order in self.orders]
        keeps, out = first_split(keep, received, firsts, self.columns.last)
        self.columns.last = keeps[:1]
        self.state[group] = keeps, self.move(out, firsts)

    def add(self, group, level):
        keeps, received = self.state[group]
        bits = [order[level + 1] for order in self.orders if level + 1 < len(order)]
        last = [] if bits else [i for i, groups in enumerate(self.gathers) if groups[-1] == group]
        earlier = [self.state[g] for i in last for g in self.gathers[i][:-1]]
        keeps, out = add_split(keeps, received, earlier, bits, self.columns.last)
        self.columns.last = keeps[:1]
        self.state[group] = (keeps, self.move(out, bits)) if bits else keeps
        for i in last:
            self.gathered[i] = keeps, self.move(keeps, [order[-1] for order in self.orders])

    def join(self, gather, level):
        left = len(self.bits) - 1 - level
        bits = [order[left] for order in self.orders]
        values = join(*self.gathered[gather], bits, 0 if left else self.chunks[1], self.columns.last)
        self.columns.last = values[:1]
        bits = [order[left - 1] for order in self.orders] if left else [1] * self.chunks[1]
        self.gathered[gather] = values, self.move(values, bits)

    def places(self):
        width, found, base = self.columns.own.shape[1], {}, 0
        for gather, groups in enumerate(self.gathers):
            sizes = [len(self.groups[g]) * width // 2 for g in groups]
            piece = self.gathered[gather][0][0].shape[1]
            for which, g in enumerate(groups):
                for index, pair in enumerate(self.groups[g]):
                    found[pair], done = [], 0
                    while done < width:
                        part, inside = divmod(index * width + done, sizes[which])
                        flat = part * sum(sizes) + sum(sizes[:which]) + inside
                        chunk, offset = divmod(flat, piece)
                        size = min(piece - offset, sizes[which] - inside, width - done)
                        found[pair].append((base + chunk, offset, done, size))
                        done += size
            base += self.chunks[1]
        return found

    def update(self, *wanted):
        blocks = self.blocks(1 + len(self.rounds))
        own, other = ([v for i in range(len(self.gathers)) for v in self.gathered[i][core]] for core in range(2))
        instead = {b: self.shares[b][0].updates[self.shares[b][1]] for b in wanted if self.shares.get(b)}
        values = update_blocks(
            blocks, self.places(), own, other, wanted, instead, self.owners, self.columns.last
        )
        self.columns.last = values[:1]
        for b, value in zip(wanted, values):
            if b and b not in self.shares or b in instead:
                step = self.columns.rounds[self.rounds[b - 1]]
                value = shift(value, [step.index(p) for p in range(self.loop)], self.fsdp)
            if b in instead:
                wave, block = self.shares[b]
                wave.updates[block] = value
            self.updates[b] = value

    def need(self, b):
        self.columns.last = self.columns.last + [self.updates[b]]

    def place(self, *wanted):
        steps = [self.columns.rounds[self.rounds[b - 1]] if b else None for b in wanted]
        tables = [sends(self.owners, step) if step else self.owners for step in steps]
        found = [(self.updates[b], table) for b, table in zip(wanted, tables)]
        columns = self.columns
        after = [value for value in columns.last if value is not columns.out]
        columns.out = place_slots(columns.out, found, columns.iterate, after)
        columns.last = [columns.out]


def body(iterate, expert_order, fsdp, loop):
    phases, waves, shares, turns = plan(loop, fsdp)
    columns = Columns(iterate, expert_order, phases, fsdp)
    waves = [Wave(columns, *wave, {}, loop, CHUNKS) for wave in waves]
    for (wave, block), (other, given) in shares.items():
        waves[wave].shares[block] = waves[other], given
        waves[other].shares[given] = None
    for turn, step, arguments in turns:
        getattr(columns if step == "send" else waves[turn], step)(*arguments)
    return columns.out


def solution(mesh):
    fsdp, loop = mesh.shape["fsdp"], mesh.shape["loop"]
    placed = (P(None, "fsdp", "loop"), P())

    def step(iterate, expert_order):
        return body(iterate, expert_order, fsdp, loop)

    return jax.shard_map(
        step, mesh=mesh, in_specs=placed, out_specs=P(None, "fsdp", "loop"), check_vma=False
    )
```

```python
import functools

import jax
import jax.numpy as jnp
from jax import lax
from jax.experimental import pallas as pl
from jax.experimental.pallas import tpu as pltpu
from jax.sharding import PartitionSpec as P

D = 7168

coef_linear = 3.4445
coef_cubic = -4.775

CHUNKS = 2, 2

MIB = 2**20
F32, BF16 = jnp.float32, jnp.bfloat16
ANY = pl.BlockSpec(memory_space=pl.ANY)
SMEM = pl.BlockSpec(memory_space=pltpu.SMEM)
VMEM = pl.BlockSpec(memory_space=pltpu.VMEM)


def plan(loop, fsdp):
    levels = fsdp.bit_length() - 2
    if loop == 4 and levels == 2:
        phases = [[[1, 3, 0, 2]], [[2, 0, 3, 1]], [[3, 1, 2, 0]], [[0, 2, 1, 3]]]
        waves = [({0: 0, 3: 3}, [[0], [1], [2]], [[0], [1, 2]], {}), ({1: 1, 2: 2}, [[0, 1], [3]], [[0, 1]], {})]
        order = [
            "0pick00", "0send0", "0pick13", "0send1", "0gram0", "0split0", "0add00", "0add01", "0send2", "0gram1",
            "0split1", "0join00", "0add10", "0join01", "0add11", "0gram2", "0send3", "0split2", "1gram0", "0add20",
            "1split0", "0add21", "1add00", "0join10", "1add01", "1gram1", "0join11", "1split1", "0update3", "1add10",
            "1add11", "1join00", "1join01", "0update120", "1update12", "0need3", "1update30", "0place0003",
            "0place0102101112", "0place13",
        ]
        turns = [(int(t[0]), t[1:].rstrip("0123456789"), [int(c) for c in t[1:] if c.isdigit()]) for t in order]
        return phases, waves, {(1, 1): (0, 1), (1, 2): (0, 2)}, turns
    rounds = [[(p + step) % loop for p in range(loop)] for step in range(1, loop)]
    turns = [(0, "pick", [0, 0]), (0, "send", [0]), (0, "gram", [0]), (0, "split", [0])]
    turns += [(0, step, [0, i]) for step in ("add", "join") for i in range(levels)]
    turns += [(0, "update", list(range(loop))), (0, "place", [i for b in range(loop) for i in (0, b)])]
    return [rounds], [({p: p for p in range(loop)}, [list(range(len(rounds)))], [[0]], {})], {}, turns


def sends(owners, step):
    return {p: owners[to] for p, to in enumerate(step) if to in owners and to != p}


def lookup(table, place):
    items = sorted(table.items())
    value = jnp.int32(items[0][1])
    for key, entry in items[1:]:
        value = jnp.where(place == key, jnp.int32(entry), value)
    return value


def struct(shape, dtype):
    return jax.ShapeDtypeStruct(shape, dtype)


def call(kernel, name, ins, specs, outs, mib, scratch=(), after=()):
    count, extra = len(ins), len(after)

    def wrapped(*refs):
        kernel(*refs[:count], *refs[count + extra :])

    result = pl.pallas_call(
        wrapped,
        out_shape=outs,
        in_specs=list(specs) + [ANY] * extra,
        out_specs=[VMEM] * len(outs),
        scratch_shapes=list(scratch),
        compiler_params=pltpu.CompilerParams(vmem_limit_bytes=int(mib * MIB)),
        cost_estimate=pl.CostEstimate(flops=0, bytes_accessed=1, transcendentals=0),
        name=name,
    )(*ins, *after)
    return list(result)


def run_copies(copies):
    for copy in copies:
        copy.start()
    for copy in copies:
        copy.wait()


def side_of(bit):
    return lax.rem(lax.div(lax.axis_index("fsdp"), bit), 2)


def is_one_of(places):
    here = lax.axis_index("loop")
    return functools.reduce(jnp.logical_or, [here == place for place in places])


def rows_at(part, height):
    return pl.ds(pl.multiple_of(part * height, height), height)


def pick(iterate, expert_order, tables, after, alone):
    def kernel(order, source, *rest):
        outs, sems = rest[:-1], rest[-1]
        place = lax.axis_index("loop")
        run_copies(
            [
                pltpu.make_async_copy(source.at[order[lookup(table, place)]], out, sems.at[i])
                for i, (table, out) in enumerate(zip(tables, outs))
            ]
        )

    outs = [struct(iterate.shape[1:], iterate.dtype)] * len(tables)
    sems = [pltpu.SemaphoreType.DMA((len(tables),))]
    return call(kernel, "pick", [expert_order, iterate], [SMEM, ANY], outs, 62 if alone else 8, sems, after=after)


def gate(value, after):
    return pl.pallas_call(
        lambda *refs: None,
        out_shape=struct(value.shape, value.dtype),
        in_specs=[ANY] * (1 + len(after)),
        out_specs=ANY,
        input_output_aliases={0: 0},
        compiler_params=pltpu.CompilerParams(vmem_limit_bytes=MIB),
        cost_estimate=pl.CostEstimate(flops=0, bytes_accessed=1, transcendentals=0),
        name="gate",
    )(value, *after)


def gram_part(blocks, pairs, chunks, owners, after):
    rows, width = blocks[0].shape
    half, count = width // 2, len(blocks)
    total = len(pairs) * width
    piece = total // chunks

    def kernel(*refs):
        xs, keep, sent, left = refs[:count], refs[count], refs[count + 1 : -1], refs[-1]
        side = side_of(1)
        pl.when(is_one_of(owners))(lambda: multiply(xs, keep, sent, left, side))

    def multiply(xs, keep, sent, left, side):
        for sending, part in ((True, 1 - side), (False, side)):
            for a in sorted({a for a, _ in pairs}):
                left[a * half : (a + 1) * half, :] = xs[a][:, rows_at(part, half)].T
            for b in sorted({b for _, b in pairs}):
                firsts = [a for a, second in pairs if second == b]
                product = jnp.dot(left[: len(firsts) * half, :], xs[b][...], preferred_element_type=F32)
                for a in firsts:
                    value = product[a * half : (a + 1) * half]
                    at = pairs.index((a, b)) * width
                    if not sending:
                        keep[:, at : at + width] = value
                        continue
                    done = 0
                    while done < width:
                        chunk, offset = divmod(at + done, piece)
                        size = min(piece - offset, width - done)
                        sent[chunk][:, offset : offset + size] = value[:, done : done + size].astype(BF16)
                        done += size

    outs = [struct((half, total), F32)] + [struct((half, piece), BF16)] * chunks
    scratch = [pltpu.VMEM((count * half, rows), BF16)]
    result = call(kernel, "gram_part", blocks, [VMEM] * count, outs, 20, scratch, after)
    return result[0], result[1:]


def first_split(keep, received, bits, after):
    rows, columns = keep.shape
    half, width = rows // 2, columns // 2
    chunks = len(received)
    piece = columns // chunks

    def kernel(kept, *refs):
        news, outs = refs[:chunks], refs[chunks:]
        for chunk, new in enumerate(news):
            i, offset = divmod(chunk * piece, width)
            side = side_of(bits[i])
            cols = slice(chunk * piece, (chunk + 1) * piece)
            for out, part in ((outs[2 + i], 1 - side), (outs[i], side)):
                at = rows_at(part, half)
                out[:, offset : offset + piece] = (kept[at, cols] + new[at, :].astype(F32)).astype(out.dtype)

    outs = [struct((half, width), F32)] * 2 + [struct((half, width), BF16)] * 2
    result = call(kernel, "first_split", [keep, *received], [VMEM] * (1 + chunks), outs, 14, after=after)
    return result[:2], result[2:]


def add_split(keeps, received, earlier, bits, after):
    count = len(keeps)
    ins_count = (2 + len(earlier)) * count
    before = sum(values[0].shape[1] for values in earlier)

    def kernel(*refs):
        ins, news, olds, outs = refs[:count], refs[count : 2 * count], refs[2 * count : ins_count], refs[ins_count:]
        for i in range(count):
            if not bits:
                done = 0
                for old in olds[i::count]:
                    outs[i][:, done : done + old.shape[1]] = old[...]
                    done += old.shape[1]
                outs[i][:, before:] = (ins[i][...] + news[i][...].astype(F32)).astype(BF16)
                continue
            half = ins[i].shape[0] // 2
            side = side_of(bits[i])
            for out, part in ((outs[count + i], 1 - side), (outs[i], side)):
                at = rows_at(part, half)
                out[...] = (ins[i][at, :] + news[i][at, :].astype(F32)).astype(out.dtype)

    if bits:
        shapes = [(k.shape[0] // 2, k.shape[1]) for k in keeps]
        outs = [struct(s, F32) for s in shapes] + [struct(s, BF16) for s in shapes]
    else:
        outs = [struct((k.shape[0], before + k.shape[1]), BF16) for k in keeps]
    ins = [*keeps, *received, *[value for values in earlier for value in values]]
    result = call(kernel, "add_split", ins, [VMEM] * ins_count, outs, 8, after=after)
    return result[:count], result[count:]


def join(values, received, bits, chunks, after):
    count = len(values)
    rows, width = values[0].shape

    def kernel(*refs):
        ins, news, outs = refs[:count], refs[count : 2 * count], refs[2 * count :]
        for i, bit in enumerate(bits):
            side = side_of(bit)
            for source, part in ((ins[i], side), (news[i], 1 - side)):
                at = rows_at(part, rows)
                if not chunks:
                    outs[i][at, :] = source[...]
                    continue
                piece = count * width // chunks
                for chunk in range(chunks):
                    low, high = max(chunk * piece, i * width), min((chunk + 1) * piece, (i + 1) * width)
                    if low < high:
                        outs[chunk][at, low - chunk * piece : high - chunk * piece] = source[
                            :, low - i * width : high - i * width
                        ]

    if chunks:
        outs = [struct((2 * rows, count * width // chunks), BF16)] * chunks
    else:
        outs = [struct((2 * rows, width), BF16)] * count
    return call(kernel, "join", [*values, *received], [VMEM] * (2 * count), outs, 8, after=after)


def swap(value, bit, fsdp, loop, places):
    pairs = [(i * loop + p, (i ^ (bit if p in places else 1)) * loop + p) for i in range(fsdp) for p in range(loop)]
    return lax.ppermute(value, ("fsdp", "loop"), pairs)


def shift(value, step, fsdp):
    loop = len(step)
    pairs = [(i * loop + p, (i ^ (to == p)) * loop + to) for i in range(fsdp) for p, to in enumerate(step)]
    return lax.ppermute(value, ("fsdp", "loop"), pairs)


def update_blocks(blocks, places, own, other, wanted, pieces, instead, owners, after):
    rows, width = blocks[0].shape
    half, count = width // 2, len(blocks)
    total, chunks = count * width, len(own)
    factor = 0.2 * D**0.5
    parts = []
    for b in wanted:
        weights, row = pieces.get(b, (1,)), 0
        for weight in weights:
            parts.append((b, row, rows * weight // sum(weights)))
            row += parts[-1][2]

    def kernel(*refs):
        xs, strips = refs[:count], (refs[count : count + chunks], refs[count + chunks : count + 2 * chunks])
        refs = refs[count + 2 * chunks :]
        given, refs = refs[: len(instead)], refs[len(instead) :]
        outs, (x, g) = refs[: len(parts)], refs[len(parts) :]
        mine = is_one_of(owners)
        pl.when(mine)(lambda: multiply(xs, strips, outs, x, g))
        for b, value in zip(instead, given):

            @pl.when(jnp.logical_not(mine))
            def _(out=outs[parts.index((b, 0, rows))], value=value):
                out[...] = value[...]

    def multiply(xs, strips, outs, x, g):
        side = side_of(1)
        for a in range(count):
            x[:, a * width : (a + 1) * width] = xs[a][...]
        for part, strip in zip((side, 1 - side), strips):
            for (a, b), pieces in places.items():
                if a not in wanted and b not in wanted:
                    continue
                where = pl.ds(pl.multiple_of(a * width + part * half, half), half)
                for chunk, offset, first, size in pieces:
                    at = b * width + first
                    g[where, at : at + size] = strip[chunk][:, offset : offset + size]
        for b in wanted:
            low, high = b * width, (b + 1) * width
            product = jnp.dot(x[:, :high], g[:high, low:high], preferred_element_type=F32)
            if b < count - 1:
                product += lax.dot_general(
                    x[:, high:], g[low:high, high:], (((1,), (1,)), ((), ())), preferred_element_type=F32
                )
            result = (factor * (coef_linear * x[:, low:high].astype(F32) + coef_cubic * product)).astype(BF16)
            for out, (block, row, height) in zip(outs, parts):
                if block == b:
                    out[...] = result[row : row + height]

    scratch = [pltpu.VMEM((rows, total), BF16), pltpu.VMEM((total, total), BF16)]
    outs = [struct((height, width), BF16) for _, _, height in parts]
    ins = [*blocks, *own, *other, *instead.values()]
    return call(kernel, "update", ins, [VMEM] * len(ins), outs, 30, scratch, after)


def place_slots(out, found, like, after):
    old = [] if out is None else [out]
    ins, cases = [], []
    for values, table in found:
        row = 0
        for value in values:
            cases += [(len(ins), place, slot, pl.ds(row, value.shape[0])) for place, slot in table.items()]
            ins.append(value)
            row += value.shape[0]

    def kernel(*refs):
        values, target, sems = refs[: len(ins)], refs[-2], refs[-1]
        here = lax.axis_index("loop")
        for wait in (False, True):
            for i, place, slot, rows in cases:

                @pl.when(here == place)
                def _(i=i, slot=slot, rows=rows):
                    copy = pltpu.make_async_copy(values[i], target.at[slot, rows], sems.at[i])
                    copy.wait() if wait else copy.start()

    return pl.pallas_call(
        kernel,
        out_shape=struct(like.shape, like.dtype),
        in_specs=[VMEM] * len(ins) + [ANY] * (len(old) + len(after)),
        out_specs=ANY,
        scratch_shapes=[pltpu.SemaphoreType.DMA((len(ins),))],
        input_output_aliases={len(ins): 0} if old else {},
        compiler_params=pltpu.CompilerParams(vmem_limit_bytes=8 * MIB),
        cost_estimate=pl.CostEstimate(flops=0, bytes_accessed=1, transcendentals=0),
        name="place_slots",
    )(*ins, *old, *after)


def back(returns):
    to = {owner: p for owners, step in returns for p, owner in enumerate(step) if owner in owners}
    places = range(len(returns[0][1]))
    rest = iter([p for p in places if p not in to.values()])
    return [to[p] if p in to else next(rest) for p in places]


class Columns:
    def __init__(self, iterate, expert_order, phases, fsdp):
        self.iterate, self.expert_order, self.phases, self.fsdp = iterate, expert_order, phases, fsdp
        self.rounds = [step for rounds in phases for step in rounds]
        self.own, self.picked, self.arrived, self.ends, self.last, self.out = None, {}, [], [0], [], None

    def pick(self, first, last):
        steps = [step for rounds in self.phases[first : last + 1] for step in rounds]
        tables = [{p: to for p, to in enumerate(step) if p != to} for step in steps]
        places = {p: p for p in range(len(steps[0]))}
        picked = pick(self.iterate, self.expert_order, tables if first else tables + [places], self.last, not first)
        if not first:
            self.own = picked.pop()
        for phase in range(first, last + 1):
            count = len(self.phases[phase])
            self.picked[phase], picked = picked[:count], picked[count:]
            self.last = self.picked[phase][:1]

    def send(self, phase):
        picked = self.picked[phase]
        if phase:
            before = self.arrived[self.ends[phase - 1] : self.ends[phase]]
            picked = [gate(value, self.last + before) for value in picked]
        self.arrived += [shift(value, step, self.fsdp) for value, step in zip(picked, self.phases[phase])]
        self.ends.append(len(self.arrived))
        self.last = picked[:1]


class Wave:
    def __init__(self, columns, owners, groups, gathers, pieces, shares, loop, chunks):
        self.columns, self.owners, self.loop, self.chunks = columns, owners, loop, chunks
        self.fsdp = columns.fsdp
        self.bits = [1 << i for i in range(1, self.fsdp.bit_length() - 1)]
        self.orders = [self.bits, self.bits[::-1]]
        self.rounds = [number for group in groups for number in group]
        self.groups, self.gathers, self.state, self.gathered, first = [], gathers, {}, {}, 0
        for group in groups:
            count = first + len(group) + 1
            self.groups.append([(a, b) for b in range(first + 1 if first else 0, count) for a in range(b + 1)])
            first += len(group)
        self.updates, self.shares, self.pieces = {b: [] for b in pieces}, shares, pieces

    def blocks(self, count):
        return [self.columns.own] + [self.columns.arrived[number] for number in self.rounds[: count - 1]]

    def move(self, values, bits):
        return [swap(value, bit, self.fsdp, self.loop, self.owners) for value, bit in zip(values, bits)]

    def gram(self, group):
        pairs = self.groups[group]
        blocks = self.blocks(1 + max(b for _, b in pairs))
        keep, out = gram_part(blocks, pairs, self.chunks[0], self.owners, self.columns.last)
        self.columns.last = [keep]
        self.state[group] = keep, self.move(out, [1] * self.chunks[0])

    def split(self, group):
        keep, received = self.state[group]
        firsts = [order[0] for order in self.orders]
        keeps, out = first_split(keep, received, firsts, self.columns.last)
        self.columns.last = keeps[:1]
        self.state[group] = keeps, self.move(out, firsts)

    def add(self, group, level):
        keeps, received = self.state[group]
        bits = [order[level + 1] for order in self.orders if level + 1 < len(order)]
        last = [] if bits else [i for i, groups in enumerate(self.gathers) if groups[-1] == group]
        earlier = [self.state[g] for i in last for g in self.gathers[i][:-1]]
        keeps, out = add_split(keeps, received, earlier, bits, self.columns.last)
        self.columns.last = keeps[:1]
        self.state[group] = (keeps, self.move(out, bits)) if bits else keeps
        for i in last:
            self.gathered[i] = keeps, self.move(keeps, [order[-1] for order in self.orders])

    def join(self, gather, level):
        left = len(self.bits) - 1 - level
        bits = [order[left] for order in self.orders]
        values = join(*self.gathered[gather], bits, 0 if left else self.chunks[1], self.columns.last)
        self.columns.last = values[:1]
        bits = [order[left - 1] for order in self.orders] if left else [1] * self.chunks[1]
        self.gathered[gather] = values, self.move(values, bits)

    def places(self):
        width, found, base = self.columns.own.shape[1], {}, 0
        for gather, groups in enumerate(self.gathers):
            sizes = [len(self.groups[g]) * width // 2 for g in groups]
            piece = self.gathered[gather][0][0].shape[1]
            for which, g in enumerate(groups):
                for index, pair in enumerate(self.groups[g]):
                    found[pair], done = [], 0
                    while done < width:
                        part, inside = divmod(index * width + done, sizes[which])
                        flat = part * sum(sizes) + sum(sizes[:which]) + inside
                        chunk, offset = divmod(flat, piece)
                        size = min(piece - offset, sizes[which] - inside, width - done)
                        found[pair].append((base + chunk, offset, done, size))
                        done += size
            base += self.chunks[1]
        return found

    def update(self, *wanted):
        blocks = self.blocks(1 + len(self.rounds))
        own, other = ([v for i in range(len(self.gathers)) for v in self.gathered[i][core]] for core in range(2))
        instead = {b: self.shares[b][0].updates[self.shares[b][1]] for b in wanted if self.shares.get(b)}
        values = update_blocks(
            blocks, self.places(), own, other, wanted, self.pieces, instead, self.owners, self.columns.last
        )
        self.columns.last = values[:1]
        for b, value in zip([b for b in wanted for _ in self.pieces.get(b, (1,))], values):
            if b and b not in self.shares or b in instead:
                returns = [self.returned(b)]
                if b in instead:
                    returns.append(self.shares[b][0].returned(self.shares[b][1]))
                value = shift(value, back(returns), self.fsdp)
            if b in instead:
                wave, block = self.shares[b]
                wave.updates[block] = value
            self.updates[b] = self.updates[b] + [value] if b in self.pieces else value

    def need(self, b):
        self.columns.last = self.columns.last + self.found(b)[0]

    def returned(self, b):
        return self.owners, self.columns.rounds[self.rounds[b - 1]]

    def found(self, b):
        value = self.updates[b]
        return value if isinstance(value, list) else [value], sends(*self.returned(b)) if b else self.owners


def body(iterate, expert_order, fsdp, loop):
    phases, waves, shares, turns = plan(loop, fsdp)
    columns = Columns(iterate, expert_order, phases, fsdp)
    waves = [Wave(columns, *wave, {}, loop, CHUNKS) for wave in waves]
    for (wave, block), (other, given) in shares.items():
        waves[wave].shares[block] = waves[other], given
        waves[other].shares[given] = None
    for turn, step, numbers in turns:
        if step == "place":
            found = [waves[wave].found(b) for wave, b in zip(numbers[::2], numbers[1::2])]
            after = [value for value in columns.last if value is not columns.out]
            columns.out = place_slots(columns.out, found, iterate, after)
            columns.last = [columns.out]
        else:
            getattr(columns if step in ("send", "pick") else waves[turn], step)(*numbers)
    return columns.out


def solution(mesh):
    fsdp, loop = mesh.shape["fsdp"], mesh.shape["loop"]
    placed = (P(None, "fsdp", "loop"), P())

    def step(iterate, expert_order):
        return body(iterate, expert_order, fsdp, loop)

    return jax.shard_map(
        step, mesh=mesh, in_specs=placed, out_specs=P(None, "fsdp", "loop"), check_vma=False
    )
```

```python
import functools

import jax
import jax.numpy as jnp
from jax import lax
from jax.experimental import pallas as pl
from jax.experimental.pallas import tpu as pltpu
from jax.sharding import PartitionSpec as P

D = 7168

coef_linear = 3.4445
coef_cubic = -4.775

MIB = 2**20
F32, BF16 = jnp.float32, jnp.bfloat16
ANY = pl.BlockSpec(memory_space=pl.ANY)
SMEM = pl.BlockSpec(memory_space=pltpu.SMEM)
VMEM = pl.BlockSpec(memory_space=pltpu.VMEM)


def plan(loop, fsdp):
    levels = fsdp.bit_length() - 2
    if loop == 4 and levels == 2:
        phases = [[[1, 3, 0, 2]], [[2, 0, 3, 1]], [[3, 1, 2, 0]], [[0, 2, 1, 3]]]
        waves = [({0: 0, 3: 3}, [[0], [1], [2]], [[0], [1, 2]], (2, 2)), ({1: 1, 2: 2}, [[0, 1], [3]], [[0, 1]], (2, 4))]
        order = [
            "0pick00", "0send0", "0pick13", "0send1", "0gram0", "0split0", "0add00", "0add01", "0send2", "0gram1",
            "0split1", "0join00", "0add10", "0join01", "0add11", "0gram2", "0send3", "0split2", "1gram0", "0add20",
            "1split0", "0add21", "1add00", "0join10", "1add01", "1gram1", "0join11", "1split1", "0update3", "1add10",
            "1add11", "1join00", "1join01", "0update120", "1update12", "0need3", "1update30", "0place0003",
            "0place0102101112", "0place13",
        ]
        turns = [(int(t[0]), t[1:].rstrip("0123456789"), [int(c) for c in t[1:] if c.isdigit()]) for t in order]
        return phases, waves, {(1, 1): (0, 1), (1, 2): (0, 2)}, turns
    rounds = [[(p + step) % loop for p in range(loop)] for step in range(1, loop)]
    turns = [(0, "pick", [0, 0]), (0, "send", [0]), (0, "gram", [0]), (0, "split", [0])]
    turns += [(0, step, [0, i]) for step in ("add", "join") for i in range(levels)]
    turns += [(0, "update", list(range(loop))), (0, "place", [i for b in range(loop) for i in (0, b)])]
    return [rounds], [({p: p for p in range(loop)}, [list(range(len(rounds)))], [[0]], (4, 4))], {}, turns


def sends(owners, step):
    return {p: owners[to] for p, to in enumerate(step) if to in owners and to != p}


def lookup(table, place):
    items = sorted(table.items())
    value = jnp.int32(items[0][1])
    for key, entry in items[1:]:
        value = jnp.where(place == key, jnp.int32(entry), value)
    return value


def struct(shape, dtype):
    return jax.ShapeDtypeStruct(shape, dtype)


def call(kernel, name, ins, specs, outs, mib, scratch=(), after=()):
    count, extra = len(ins), len(after)

    def wrapped(*refs):
        kernel(*refs[:count], *refs[count + extra :])

    result = pl.pallas_call(
        wrapped,
        out_shape=outs,
        in_specs=list(specs) + [ANY] * extra,
        out_specs=[VMEM] * len(outs),
        scratch_shapes=list(scratch),
        compiler_params=pltpu.CompilerParams(vmem_limit_bytes=int(mib * MIB)),
        cost_estimate=pl.CostEstimate(flops=0, bytes_accessed=1, transcendentals=0),
        name=name,
    )(*ins, *after)
    return list(result)


def run_copies(copies):
    for copy in copies:
        copy.start()
    for copy in copies:
        copy.wait()


def side_of(bit):
    return lax.rem(lax.div(lax.axis_index("fsdp"), bit), 2)


def is_one_of(places):
    here = lax.axis_index("loop")
    return functools.reduce(jnp.logical_or, [here == place for place in places])


def rows_at(part, height):
    return pl.ds(pl.multiple_of(part * height, height), height)


def pick(iterate, expert_order, tables, after, alone):
    def kernel(order, source, *rest):
        outs, sems = rest[:-1], rest[-1]
        place = lax.axis_index("loop")
        run_copies(
            [
                pltpu.make_async_copy(source.at[order[lookup(table, place)]], out, sems.at[i])
                for i, (table, out) in enumerate(zip(tables, outs))
            ]
        )

    outs = [struct(iterate.shape[1:], iterate.dtype)] * len(tables)
    sems = [pltpu.SemaphoreType.DMA((len(tables),))]
    return call(kernel, "pick", [expert_order, iterate], [SMEM, ANY], outs, 62 if alone else 8, sems, after=after)


def gate(value, after):
    return pl.pallas_call(
        lambda *refs: None,
        out_shape=struct(value.shape, value.dtype),
        in_specs=[ANY] * (1 + len(after)),
        out_specs=ANY,
        input_output_aliases={0: 0},
        compiler_params=pltpu.CompilerParams(vmem_limit_bytes=MIB),
        cost_estimate=pl.CostEstimate(flops=0, bytes_accessed=1, transcendentals=0),
        name="gate",
    )(value, *after)


def gram_part(blocks, pairs, chunks, owners, after):
    rows, width = blocks[0].shape
    half, count = width // 2, len(blocks)
    total = len(pairs) * width
    piece = total // chunks

    def kernel(*refs):
        xs, keep, sent, left = refs[:count], refs[count], refs[count + 1 : -1], refs[-1]
        side = side_of(1)
        pl.when(is_one_of(owners))(lambda: multiply(xs, keep, sent, left, side))

    def multiply(xs, keep, sent, left, side):
        for sending, part in ((True, 1 - side), (False, side)):
            for a in sorted({a for a, _ in pairs}):
                left[a * half : (a + 1) * half, :] = xs[a][:, rows_at(part, half)].T
            for b in sorted({b for _, b in pairs}):
                firsts = [a for a, second in pairs if second == b]
                product = jnp.dot(left[: len(firsts) * half, :], xs[b][...], preferred_element_type=F32)
                for a in firsts:
                    value = product[a * half : (a + 1) * half]
                    at = pairs.index((a, b)) * width
                    if not sending:
                        keep[:, at : at + width] = value
                        continue
                    done = 0
                    while done < width:
                        chunk, offset = divmod(at + done, piece)
                        size = min(piece - offset, width - done)
                        sent[chunk][:, offset : offset + size] = value[:, done : done + size].astype(BF16)
                        done += size

    outs = [struct((half, total), F32)] + [struct((half, piece), BF16)] * chunks
    scratch = [pltpu.VMEM((count * half, rows), BF16)]
    result = call(kernel, "gram_part", blocks, [VMEM] * count, outs, 20, scratch, after)
    return result[0], result[1:]


def first_split(keep, received, bits, after):
    rows, columns = keep.shape
    half, width = rows // 2, columns // 2
    chunks = len(received)
    piece = columns // chunks

    def kernel(kept, *refs):
        news, outs = refs[:chunks], refs[chunks:]
        for chunk, new in enumerate(news):
            i, offset = divmod(chunk * piece, width)
            side = side_of(bits[i])
            cols = slice(chunk * piece, (chunk + 1) * piece)
            for out, part in ((outs[2 + i], 1 - side), (outs[i], side)):
                at = rows_at(part, half)
                out[:, offset : offset + piece] = (kept[at, cols] + new[at, :].astype(F32)).astype(out.dtype)

    outs = [struct((half, width), F32)] * 2 + [struct((half, width), BF16)] * 2
    result = call(kernel, "first_split", [keep, *received], [VMEM] * (1 + chunks), outs, 14, after=after)
    return result[:2], result[2:]


def add_split(keeps, received, earlier, bits, after):
    count = len(keeps)
    ins_count = (2 + len(earlier)) * count
    before = sum(values[0].shape[1] for values in earlier)

    def kernel(*refs):
        ins, news, olds, outs = refs[:count], refs[count : 2 * count], refs[2 * count : ins_count], refs[ins_count:]
        for i in range(count):
            if not bits:
                done = 0
                for old in olds[i::count]:
                    outs[i][:, done : done + old.shape[1]] = old[...]
                    done += old.shape[1]
                outs[i][:, before:] = (ins[i][...] + news[i][...].astype(F32)).astype(BF16)
                continue
            half = ins[i].shape[0] // 2
            side = side_of(bits[i])
            for out, part in ((outs[count + i], 1 - side), (outs[i], side)):
                at = rows_at(part, half)
                out[...] = (ins[i][at, :] + news[i][at, :].astype(F32)).astype(out.dtype)

    if bits:
        shapes = [(k.shape[0] // 2, k.shape[1]) for k in keeps]
        outs = [struct(s, F32) for s in shapes] + [struct(s, BF16) for s in shapes]
    else:
        outs = [struct((k.shape[0], before + k.shape[1]), BF16) for k in keeps]
    ins = [*keeps, *received, *[value for values in earlier for value in values]]
    result = call(kernel, "add_split", ins, [VMEM] * ins_count, outs, 8, after=after)
    return result[:count], result[count:]


def join(values, received, bits, chunks, after):
    count = len(values)
    rows, width = values[0].shape

    def kernel(*refs):
        ins, news, outs = refs[:count], refs[count : 2 * count], refs[2 * count :]
        for i, bit in enumerate(bits):
            side = side_of(bit)
            for source, part in ((ins[i], side), (news[i], 1 - side)):
                at = rows_at(part, rows)
                if not chunks:
                    outs[i][at, :] = source[...]
                    continue
                piece = count * width // chunks
                for chunk in range(chunks):
                    low, high = max(chunk * piece, i * width), min((chunk + 1) * piece, (i + 1) * width)
                    if low < high:
                        outs[chunk][at, low - chunk * piece : high - chunk * piece] = source[
                            :, low - i * width : high - i * width
                        ]

    if chunks:
        outs = [struct((2 * rows, count * width // chunks), BF16)] * chunks
    else:
        outs = [struct((2 * rows, width), BF16)] * count
    return call(kernel, "join", [*values, *received], [VMEM] * (2 * count), outs, 8, after=after)


def swap(value, bit, fsdp, loop, places):
    pairs = [(i * loop + p, (i ^ (bit if p in places else 1)) * loop + p) for i in range(fsdp) for p in range(loop)]
    return lax.ppermute(value, ("fsdp", "loop"), pairs)


def shift(value, step, fsdp):
    loop = len(step)
    pairs = [(i * loop + p, (i ^ (to == p)) * loop + to) for i in range(fsdp) for p, to in enumerate(step)]
    return lax.ppermute(value, ("fsdp", "loop"), pairs)


def update_blocks(blocks, places, own, other, wanted, instead, owners, after):
    rows, width = blocks[0].shape
    half, count = width // 2, len(blocks)
    total, chunks = count * width, len(own)
    factor = 0.2 * D**0.5

    def kernel(*refs):
        xs, strips = refs[:count], (refs[count : count + chunks], refs[count + chunks : count + 2 * chunks])
        refs = refs[count + 2 * chunks :]
        given, refs = refs[: len(instead)], refs[len(instead) :]
        outs, (x, g) = refs[: len(wanted)], refs[len(wanted) :]
        mine = is_one_of(owners)
        pl.when(mine)(lambda: multiply(xs, strips, outs, x, g))
        for b, value in zip(instead, given):

            @pl.when(jnp.logical_not(mine))
            def _(out=outs[wanted.index(b)], value=value):
                out[...] = value[...]

    def multiply(xs, strips, outs, x, g):
        side = side_of(1)
        for a in range(count):
            x[:, a * width : (a + 1) * width] = xs[a][...]
        for part, strip in zip((side, 1 - side), strips):
            for (a, b), pieces in places.items():
                if a not in wanted and b not in wanted:
                    continue
                where = pl.ds(pl.multiple_of(a * width + part * half, half), half)
                for chunk, offset, first, size in pieces:
                    at = b * width + first
                    g[where, at : at + size] = strip[chunk][:, offset : offset + size]
        for out, b in zip(outs, wanted):
            low, high = b * width, (b + 1) * width
            product = jnp.dot(x[:, :high], g[:high, low:high], preferred_element_type=F32)
            if b < count - 1:
                product += lax.dot_general(
                    x[:, high:], g[low:high, high:], (((1,), (1,)), ((), ())), preferred_element_type=F32
                )
            out[...] = (factor * (coef_linear * x[:, low:high].astype(F32) + coef_cubic * product)).astype(BF16)

    scratch = [pltpu.VMEM((rows, total), BF16), pltpu.VMEM((total, total), BF16)]
    outs = [struct((rows, width), BF16)] * len(wanted)
    ins = [*blocks, *own, *other, *instead.values()]
    return call(kernel, "update", ins, [VMEM] * len(ins), outs, 30, scratch, after)


def place_slots(out, found, like, after):
    old = [] if out is None else [out]
    ins = [value for value, _ in found]
    cases = [(i, place, slot) for i, (_, table) in enumerate(found) for place, slot in table.items()]

    def kernel(*refs):
        values, target, sems = refs[: len(ins)], refs[-2], refs[-1]
        here = lax.axis_index("loop")
        for wait in (False, True):
            for i, place, slot in cases:

                @pl.when(here == place)
                def _(i=i, slot=slot):
                    copy = pltpu.make_async_copy(values[i], target.at[slot], sems.at[i])
                    copy.wait() if wait else copy.start()

    return pl.pallas_call(
        kernel,
        out_shape=struct(like.shape, like.dtype),
        in_specs=[VMEM] * len(ins) + [ANY] * (len(old) + len(after)),
        out_specs=ANY,
        scratch_shapes=[pltpu.SemaphoreType.DMA((len(ins),))],
        input_output_aliases={len(ins): 0} if old else {},
        compiler_params=pltpu.CompilerParams(vmem_limit_bytes=8 * MIB),
        cost_estimate=pl.CostEstimate(flops=0, bytes_accessed=1, transcendentals=0),
        name="place_slots",
    )(*ins, *old, *after)


def back(returns):
    to = {owner: p for owners, step in returns for p, owner in enumerate(step) if owner in owners}
    places = range(len(returns[0][1]))
    rest = iter([p for p in places if p not in to.values()])
    return [to[p] if p in to else next(rest) for p in places]


class Columns:
    def __init__(self, iterate, expert_order, phases, fsdp):
        self.iterate, self.expert_order, self.phases, self.fsdp = iterate, expert_order, phases, fsdp
        self.rounds = [step for rounds in phases for step in rounds]
        self.own, self.picked, self.arrived, self.ends, self.last, self.out = None, {}, [], [0], [], None

    def pick(self, first, last):
        steps = [step for rounds in self.phases[first : last + 1] for step in rounds]
        tables = [{p: to for p, to in enumerate(step) if p != to} for step in steps]
        places = {p: p for p in range(len(steps[0]))}
        picked = pick(self.iterate, self.expert_order, tables if first else tables + [places], self.last, not first)
        if not first:
            self.own = picked.pop()
        for phase in range(first, last + 1):
            count = len(self.phases[phase])
            self.picked[phase], picked = picked[:count], picked[count:]
            self.last = self.picked[phase][:1]

    def send(self, phase):
        picked = self.picked[phase]
        if phase:
            before = self.arrived[self.ends[phase - 1] : self.ends[phase]]
            picked = [gate(value, self.last + before) for value in picked]
        self.arrived += [shift(value, step, self.fsdp) for value, step in zip(picked, self.phases[phase])]
        self.ends.append(len(self.arrived))
        self.last = picked[:1]


class Wave:
    def __init__(self, columns, owners, groups, gathers, chunks, loop):
        self.columns, self.owners, self.loop, self.chunks = columns, owners, loop, chunks
        self.fsdp = columns.fsdp
        self.bits = [1 << i for i in range(1, self.fsdp.bit_length() - 1)]
        self.orders = [self.bits, self.bits[::-1]]
        self.rounds = [number for group in groups for number in group]
        self.groups, self.gathers, self.state, self.gathered, first = [], gathers, {}, {}, 0
        for group in groups:
            count = first + len(group) + 1
            self.groups.append([(a, b) for b in range(first + 1 if first else 0, count) for a in range(b + 1)])
            first += len(group)
        self.updates, self.shares = {}, {}

    def blocks(self, count):
        return [self.columns.own] + [self.columns.arrived[number] for number in self.rounds[: count - 1]]

    def move(self, values, bits):
        return [swap(value, bit, self.fsdp, self.loop, self.owners) for value, bit in zip(values, bits)]

    def gram(self, group):
        pairs = self.groups[group]
        blocks = self.blocks(1 + max(b for _, b in pairs))
        keep, out = gram_part(blocks, pairs, self.chunks[0], self.owners, self.columns.last)
        self.columns.last = [keep]
        self.state[group] = keep, self.move(out, [1] * self.chunks[0])

    def split(self, group):
        keep, received = self.state[group]
        firsts = [order[0] for order in self.orders]
        keeps, out = first_split(keep, received, firsts, self.columns.last)
        self.columns.last = keeps[:1]
        self.state[group] = keeps, self.move(out, firsts)

    def add(self, group, level):
        keeps, received = self.state[group]
        bits = [order[level + 1] for order in self.orders if level + 1 < len(order)]
        last = [] if bits else [i for i, groups in enumerate(self.gathers) if groups[-1] == group]
        earlier = [self.state[g] for i in last for g in self.gathers[i][:-1]]
        keeps, out = add_split(keeps, received, earlier, bits, self.columns.last)
        self.columns.last = keeps[:1]
        self.state[group] = (keeps, self.move(out, bits)) if bits else keeps
        for i in last:
            self.gathered[i] = keeps, self.move(keeps, [order[-1] for order in self.orders])

    def join(self, gather, level):
        left = len(self.bits) - 1 - level
        bits = [order[left] for order in self.orders]
        values = join(*self.gathered[gather], bits, 0 if left else self.chunks[1], self.columns.last)
        self.columns.last = values[:1]
        bits = [order[left - 1] for order in self.orders] if left else [1] * self.chunks[1]
        self.gathered[gather] = values, self.move(values, bits)

    def places(self):
        width, found, base = self.columns.own.shape[1], {}, 0
        for gather, groups in enumerate(self.gathers):
            sizes = [len(self.groups[g]) * width // 2 for g in groups]
            piece = self.gathered[gather][0][0].shape[1]
            for which, g in enumerate(groups):
                for index, pair in enumerate(self.groups[g]):
                    found[pair], done = [], 0
                    while done < width:
                        part, inside = divmod(index * width + done, sizes[which])
                        flat = part * sum(sizes) + sum(sizes[:which]) + inside
                        chunk, offset = divmod(flat, piece)
                        size = min(piece - offset, sizes[which] - inside, width - done)
                        found[pair].append((base + chunk, offset, done, size))
                        done += size
            base += self.chunks[1]
        return found

    def update(self, *wanted):
        blocks = self.blocks(1 + len(self.rounds))
        own, other = ([v for i in range(len(self.gathers)) for v in self.gathered[i][core]] for core in range(2))
        instead = {b: self.shares[b][0].updates[self.shares[b][1]] for b in wanted if self.shares.get(b)}
        values = update_blocks(
            blocks, self.places(), own, other, wanted, instead, self.owners, self.columns.last
        )
        self.columns.last = values[:1]
        for b, value in zip(wanted, values):
            if b and b not in self.shares or b in instead:
                returns = [self.returned(b)]
                if b in instead:
                    returns.append(self.shares[b][0].returned(self.shares[b][1]))
                value = shift(value, back(returns), self.fsdp)
            if b in instead:
                wave, block = self.shares[b]
                wave.updates[block] = value
            self.updates[b] = value

    def need(self, b):
        self.columns.last = self.columns.last + [self.updates[b]]

    def returned(self, b):
        return self.owners, self.columns.rounds[self.rounds[b - 1]]

    def found(self, b):
        return self.updates[b], sends(*self.returned(b)) if b else self.owners


def body(iterate, expert_order, fsdp, loop):
    phases, waves, shares, turns = plan(loop, fsdp)
    columns = Columns(iterate, expert_order, phases, fsdp)
    waves = [Wave(columns, *wave, loop) for wave in waves]
    for (wave, block), (other, given) in shares.items():
        waves[wave].shares[block] = waves[other], given
        waves[other].shares[given] = None
    for turn, step, numbers in turns:
        if step == "place":
            found = [waves[wave].found(b) for wave, b in zip(numbers[::2], numbers[1::2])]
            after = [value for value in columns.last if value is not columns.out]
            columns.out = place_slots(columns.out, found, iterate, after)
            columns.last = [columns.out]
        else:
            getattr(columns if step in ("send", "pick") else waves[turn], step)(*numbers)
    return columns.out


def solution(mesh):
    fsdp, loop = mesh.shape["fsdp"], mesh.shape["loop"]
    placed = (P(None, "fsdp", "loop"), P())

    def step(iterate, expert_order):
        return body(iterate, expert_order, fsdp, loop)

    return jax.shard_map(
        step, mesh=mesh, in_specs=placed, out_specs=P(None, "fsdp", "loop"), check_vma=False
    )
```

```python
import functools

import jax
import jax.numpy as jnp
from jax import lax
from jax.experimental import pallas as pl
from jax.experimental.pallas import tpu as pltpu
from jax.sharding import PartitionSpec as P

D = 7168

coef_linear = 3.4445
coef_cubic = -4.775

MIB = 2**20
F32, BF16 = jnp.float32, jnp.bfloat16
ANY = pl.BlockSpec(memory_space=pl.ANY)
SMEM = pl.BlockSpec(memory_space=pltpu.SMEM)
VMEM = pl.BlockSpec(memory_space=pltpu.VMEM)


def plan(loop, fsdp):
    levels = fsdp.bit_length() - 2
    if loop == 4 and levels == 2:
        phases = [[[1, 3, 0, 2]], [[2, 0, 3, 1]], [[3, 1, 2, 0]], [[0, 2, 1, 3]]]
        waves = [({0: 0, 3: 3}, [[0], [1], [2]], [[0], [1, 2]], (2, 2)), ({1: 1, 2: 2}, [[0, 1], [3]], [[0, 1]], (2, 4))]
        order = [
            "0pick00", "0send0", "0pick13", "0send1", "0gram0", "0split0", "0add00", "0add01", "0send2", "0gram1",
            "0split1", "0join00", "0add10", "0join01", "0add11", "0gram2", "0send3", "0split2", "1gram0", "0add20",
            "1split0", "0add21", "1add00", "0join10", "1add01", "1gram1", "0join11", "1split1", "1add10", "0update3",
            "1add11", "1join00", "1join01", "0update120", "1update12", "0need3", "1update30", "0place0003",
            "0place0102101112", "0place13",
        ]
        turns = [(int(t[0]), t[1:].rstrip("0123456789"), [int(c) for c in t[1:] if c.isdigit()]) for t in order]
        return phases, waves, {(1, 1): (0, 1), (1, 2): (0, 2)}, turns
    rounds = [[(p + step) % loop for p in range(loop)] for step in range(1, loop)]
    turns = [(0, "pick", [0, 0]), (0, "send", [0]), (0, "gram", [0]), (0, "split", [0])]
    turns += [(0, step, [0, i]) for step in ("add", "join") for i in range(levels)]
    turns += [(0, "update", list(range(loop))), (0, "place", [i for b in range(loop) for i in (0, b)])]
    return [rounds], [({p: p for p in range(loop)}, [list(range(len(rounds)))], [[0]], (4, 4))], {}, turns


def sends(owners, step):
    return {p: owners[to] for p, to in enumerate(step) if to in owners and to != p}


def lookup(table, place):
    items = sorted(table.items())
    value = jnp.int32(items[0][1])
    for key, entry in items[1:]:
        value = jnp.where(place == key, jnp.int32(entry), value)
    return value


def struct(shape, dtype):
    return jax.ShapeDtypeStruct(shape, dtype)


def call(kernel, name, ins, specs, outs, mib, scratch=(), after=()):
    count, extra = len(ins), len(after)

    def wrapped(*refs):
        kernel(*refs[:count], *refs[count + extra :])

    result = pl.pallas_call(
        wrapped,
        out_shape=outs,
        in_specs=list(specs) + [ANY] * extra,
        out_specs=[VMEM] * len(outs),
        scratch_shapes=list(scratch),
        compiler_params=pltpu.CompilerParams(vmem_limit_bytes=int(mib * MIB)),
        cost_estimate=pl.CostEstimate(flops=0, bytes_accessed=1, transcendentals=0),
        name=name,
    )(*ins, *after)
    return list(result)


def run_copies(copies):
    for copy in copies:
        copy.start()
    for copy in copies:
        copy.wait()


def side_of(bit):
    return lax.rem(lax.div(lax.axis_index("fsdp"), bit), 2)


def is_one_of(places):
    here = lax.axis_index("loop")
    return functools.reduce(jnp.logical_or, [here == place for place in places])


def rows_at(part, height):
    return pl.ds(pl.multiple_of(part * height, height), height)


def pick(iterate, expert_order, tables, after, alone):
    def kernel(order, source, *rest):
        outs, sems = rest[:-1], rest[-1]
        place = lax.axis_index("loop")
        run_copies(
            [
                pltpu.make_async_copy(source.at[order[lookup(table, place)]], out, sems.at[i])
                for i, (table, out) in enumerate(zip(tables, outs))
            ]
        )

    outs = [struct(iterate.shape[1:], iterate.dtype)] * len(tables)
    sems = [pltpu.SemaphoreType.DMA((len(tables),))]
    return call(kernel, "pick", [expert_order, iterate], [SMEM, ANY], outs, 62 if alone else 8, sems, after=after)


def gate(value, after):
    return pl.pallas_call(
        lambda *refs: None,
        out_shape=struct(value.shape, value.dtype),
        in_specs=[ANY] * (1 + len(after)),
        out_specs=ANY,
        input_output_aliases={0: 0},
        compiler_params=pltpu.CompilerParams(vmem_limit_bytes=MIB),
        cost_estimate=pl.CostEstimate(flops=0, bytes_accessed=1, transcendentals=0),
        name="gate",
    )(value, *after)


def gram_part(blocks, pairs, chunks, owners, after):
    rows, width = blocks[0].shape
    half, count = width // 2, len(blocks)
    total = len(pairs) * width
    piece = total // chunks

    def kernel(*refs):
        xs, keep, sent, left = refs[:count], refs[count], refs[count + 1 : -1], refs[-1]
        side = side_of(1)
        pl.when(is_one_of(owners))(lambda: multiply(xs, keep, sent, left, side))

    def multiply(xs, keep, sent, left, side):
        for sending, part in ((True, 1 - side), (False, side)):
            for a in sorted({a for a, _ in pairs}):
                left[a * half : (a + 1) * half, :] = xs[a][:, rows_at(part, half)].T
            for b in sorted({b for _, b in pairs}):
                firsts = [a for a, second in pairs if second == b]
                product = jnp.dot(left[: len(firsts) * half, :], xs[b][...], preferred_element_type=F32)
                for a in firsts:
                    value = product[a * half : (a + 1) * half]
                    at = pairs.index((a, b)) * width
                    if not sending:
                        keep[:, at : at + width] = value
                        continue
                    done = 0
                    while done < width:
                        chunk, offset = divmod(at + done, piece)
                        size = min(piece - offset, width - done)
                        sent[chunk][:, offset : offset + size] = value[:, done : done + size].astype(BF16)
                        done += size

    outs = [struct((half, total), F32)] + [struct((half, piece), BF16)] * chunks
    scratch = [pltpu.VMEM((count * half, rows), BF16)]
    result = call(kernel, "gram_part", blocks, [VMEM] * count, outs, 20, scratch, after)
    return result[0], result[1:]


def first_split(keep, received, bits, after):
    rows, columns = keep.shape
    half, width = rows // 2, columns // 2
    chunks = len(received)
    piece = columns // chunks

    def kernel(kept, *refs):
        news, outs = refs[:chunks], refs[chunks:]
        for chunk, new in enumerate(news):
            i, offset = divmod(chunk * piece, width)
            side = side_of(bits[i])
            cols = slice(chunk * piece, (chunk + 1) * piece)
            for out, part in ((outs[2 + i], 1 - side), (outs[i], side)):
                at = rows_at(part, half)
                out[:, offset : offset + piece] = (kept[at, cols] + new[at, :].astype(F32)).astype(out.dtype)

    outs = [struct((half, width), F32)] * 2 + [struct((half, width), BF16)] * 2
    result = call(kernel, "first_split", [keep, *received], [VMEM] * (1 + chunks), outs, 14, after=after)
    return result[:2], result[2:]


def add_split(keeps, received, earlier, bits, after):
    count = len(keeps)
    ins_count = (2 + len(earlier)) * count
    before = sum(values[0].shape[1] for values in earlier)

    def kernel(*refs):
        ins, news, olds, outs = refs[:count], refs[count : 2 * count], refs[2 * count : ins_count], refs[ins_count:]
        for i in range(count):
            if not bits:
                done = 0
                for old in olds[i::count]:
                    outs[i][:, done : done + old.shape[1]] = old[...]
                    done += old.shape[1]
                outs[i][:, before:] = (ins[i][...] + news[i][...].astype(F32)).astype(BF16)
                continue
            half = ins[i].shape[0] // 2
            side = side_of(bits[i])
            for out, part in ((outs[count + i], 1 - side), (outs[i], side)):
                at = rows_at(part, half)
                out[...] = (ins[i][at, :] + news[i][at, :].astype(F32)).astype(out.dtype)

    if bits:
        shapes = [(k.shape[0] // 2, k.shape[1]) for k in keeps]
        outs = [struct(s, F32) for s in shapes] + [struct(s, BF16) for s in shapes]
    else:
        outs = [struct((k.shape[0], before + k.shape[1]), BF16) for k in keeps]
    ins = [*keeps, *received, *[value for values in earlier for value in values]]
    result = call(kernel, "add_split", ins, [VMEM] * ins_count, outs, 8, after=after)
    return result[:count], result[count:]


def join(values, received, bits, chunks, after):
    count = len(values)
    rows, width = values[0].shape

    def kernel(*refs):
        ins, news, outs = refs[:count], refs[count : 2 * count], refs[2 * count :]
        for i, bit in enumerate(bits):
            side = side_of(bit)
            for source, part in ((ins[i], side), (news[i], 1 - side)):
                at = rows_at(part, rows)
                if not chunks:
                    outs[i][at, :] = source[...]
                    continue
                piece = count * width // chunks
                for chunk in range(chunks):
                    low, high = max(chunk * piece, i * width), min((chunk + 1) * piece, (i + 1) * width)
                    if low < high:
                        outs[chunk][at, low - chunk * piece : high - chunk * piece] = source[
                            :, low - i * width : high - i * width
                        ]

    if chunks:
        outs = [struct((2 * rows, count * width // chunks), BF16)] * chunks
    else:
        outs = [struct((2 * rows, width), BF16)] * count
    return call(kernel, "join", [*values, *received], [VMEM] * (2 * count), outs, 8, after=after)


def swap(value, bit, fsdp, loop, places):
    pairs = [(i * loop + p, (i ^ (bit if p in places else 1)) * loop + p) for i in range(fsdp) for p in range(loop)]
    return lax.ppermute(value, ("fsdp", "loop"), pairs)


def shift(value, step, fsdp):
    loop = len(step)
    pairs = [(i * loop + p, (i ^ (to == p)) * loop + to) for i in range(fsdp) for p, to in enumerate(step)]
    return lax.ppermute(value, ("fsdp", "loop"), pairs)


def update_blocks(blocks, places, own, other, wanted, instead, owners, after):
    rows, width = blocks[0].shape
    half, count = width // 2, len(blocks)
    total, chunks = count * width, len(own)
    factor = 0.2 * D**0.5

    def kernel(*refs):
        xs, strips = refs[:count], (refs[count : count + chunks], refs[count + chunks : count + 2 * chunks])
        refs = refs[count + 2 * chunks :]
        given, refs = refs[: len(instead)], refs[len(instead) :]
        outs, (x, g) = refs[: len(wanted)], refs[len(wanted) :]
        mine = is_one_of(owners)
        pl.when(mine)(lambda: multiply(xs, strips, outs, x, g))
        for b, value in zip(instead, given):

            @pl.when(jnp.logical_not(mine))
            def _(out=outs[wanted.index(b)], value=value):
                out[...] = value[...]

    def multiply(xs, strips, outs, x, g):
        side = side_of(1)
        for a in range(count):
            x[:, a * width : (a + 1) * width] = xs[a][...]
        for part, strip in zip((side, 1 - side), strips):
            for (a, b), pieces in places.items():
                if a not in wanted and b not in wanted:
                    continue
                where = pl.ds(pl.multiple_of(a * width + part * half, half), half)
                for chunk, offset, first, size in pieces:
                    at = b * width + first
                    g[where, at : at + size] = strip[chunk][:, offset : offset + size]
        for out, b in zip(outs, wanted):
            low, high = b * width, (b + 1) * width
            product = jnp.dot(x[:, :high], g[:high, low:high], preferred_element_type=F32)
            if b < count - 1:
                product += lax.dot_general(
                    x[:, high:], g[low:high, high:], (((1,), (1,)), ((), ())), preferred_element_type=F32
                )
            out[...] = (factor * (coef_linear * x[:, low:high].astype(F32) + coef_cubic * product)).astype(BF16)

    scratch = [pltpu.VMEM((rows, total), BF16), pltpu.VMEM((total, total), BF16)]
    outs = [struct((rows, width), BF16)] * len(wanted)
    ins = [*blocks, *own, *other, *instead.values()]
    return call(kernel, "update", ins, [VMEM] * len(ins), outs, 30, scratch, after)


def place_slots(out, found, like, after):
    old = [] if out is None else [out]
    ins = [value for value, _ in found]
    cases = [(i, place, slot) for i, (_, table) in enumerate(found) for place, slot in table.items()]

    def kernel(*refs):
        values, target, sems = refs[: len(ins)], refs[-2], refs[-1]
        here = lax.axis_index("loop")
        for wait in (False, True):
            for i, place, slot in cases:

                @pl.when(here == place)
                def _(i=i, slot=slot):
                    copy = pltpu.make_async_copy(values[i], target.at[slot], sems.at[i])
                    copy.wait() if wait else copy.start()

    return pl.pallas_call(
        kernel,
        out_shape=struct(like.shape, like.dtype),
        in_specs=[VMEM] * len(ins) + [ANY] * (len(old) + len(after)),
        out_specs=ANY,
        scratch_shapes=[pltpu.SemaphoreType.DMA((len(ins),))],
        input_output_aliases={len(ins): 0} if old else {},
        compiler_params=pltpu.CompilerParams(vmem_limit_bytes=8 * MIB),
        cost_estimate=pl.CostEstimate(flops=0, bytes_accessed=1, transcendentals=0),
        name="place_slots",
    )(*ins, *old, *after)


def back(returns):
    to = {owner: p for owners, step in returns for p, owner in enumerate(step) if owner in owners}
    places = range(len(returns[0][1]))
    rest = iter([p for p in places if p not in to.values()])
    return [to[p] if p in to else next(rest) for p in places]


class Columns:
    def __init__(self, iterate, expert_order, phases, fsdp):
        self.iterate, self.expert_order, self.phases, self.fsdp = iterate, expert_order, phases, fsdp
        self.rounds = [step for rounds in phases for step in rounds]
        self.own, self.picked, self.arrived, self.ends, self.last, self.out = None, {}, [], [0], [], None

    def pick(self, first, last):
        steps = [step for rounds in self.phases[first : last + 1] for step in rounds]
        tables = [{p: to for p, to in enumerate(step) if p != to} for step in steps]
        places = {p: p for p in range(len(steps[0]))}
        ends = last == len(self.phases) - 1
        tables = tables + [places] if ends else tables
        picked = pick(self.iterate, self.expert_order, tables, self.last, not first)
        if ends:
            self.own = picked.pop()
        for phase in range(first, last + 1):
            count = len(self.phases[phase])
            self.picked[phase], picked = picked[:count], picked[count:]
            self.last = self.picked[phase][:1]

    def send(self, phase):
        picked = self.picked[phase]
        if phase:
            before = self.arrived[self.ends[phase - 1] : self.ends[phase]]
            picked = [gate(value, self.last + before) for value in picked]
        self.arrived += [shift(value, step, self.fsdp) for value, step in zip(picked, self.phases[phase])]
        self.ends.append(len(self.arrived))
        self.last = picked[:1]


class Wave:
    def __init__(self, columns, owners, groups, gathers, chunks, loop):
        self.columns, self.owners, self.loop, self.chunks = columns, owners, loop, chunks
        self.fsdp = columns.fsdp
        self.bits = [1 << i for i in range(1, self.fsdp.bit_length() - 1)]
        self.orders = [self.bits, self.bits[::-1]]
        self.rounds = [number for group in groups for number in group]
        self.groups, self.gathers, self.state, self.gathered, first = [], gathers, {}, {}, 0
        for group in groups:
            count = first + len(group) + 1
            self.groups.append([(a, b) for b in range(first + 1 if first else 0, count) for a in range(b + 1)])
            first += len(group)
        self.updates, self.shares = {}, {}

    def blocks(self, count):
        return [self.columns.own] + [self.columns.arrived[number] for number in self.rounds[: count - 1]]

    def move(self, values, bits):
        return [swap(value, bit, self.fsdp, self.loop, self.owners) for value, bit in zip(values, bits)]

    def gram(self, group):
        pairs = self.groups[group]
        blocks = self.blocks(1 + max(b for _, b in pairs))
        keep, out = gram_part(blocks, pairs, self.chunks[0], self.owners, self.columns.last)
        self.columns.last = [keep]
        self.state[group] = keep, self.move(out, [1] * self.chunks[0])

    def split(self, group):
        keep, received = self.state[group]
        firsts = [order[0] for order in self.orders]
        keeps, out = first_split(keep, received, firsts, self.columns.last)
        self.columns.last = keeps[:1]
        self.state[group] = keeps, self.move(out, firsts)

    def add(self, group, level):
        keeps, received = self.state[group]
        bits = [order[level + 1] for order in self.orders if level + 1 < len(order)]
        last = [] if bits else [i for i, groups in enumerate(self.gathers) if groups[-1] == group]
        earlier = [self.state[g] for i in last for g in self.gathers[i][:-1]]
        keeps, out = add_split(keeps, received, earlier, bits, self.columns.last)
        self.columns.last = keeps[:1]
        self.state[group] = (keeps, self.move(out, bits)) if bits else keeps
        for i in last:
            self.gathered[i] = keeps, self.move(keeps, [order[-1] for order in self.orders])

    def join(self, gather, level):
        left = len(self.bits) - 1 - level
        bits = [order[left] for order in self.orders]
        values = join(*self.gathered[gather], bits, 0 if left else self.chunks[1], self.columns.last)
        self.columns.last = values[:1]
        bits = [order[left - 1] for order in self.orders] if left else [1] * self.chunks[1]
        self.gathered[gather] = values, self.move(values, bits)

    def places(self):
        width, found, base = self.columns.own.shape[1], {}, 0
        for gather, groups in enumerate(self.gathers):
            sizes = [len(self.groups[g]) * width // 2 for g in groups]
            piece = self.gathered[gather][0][0].shape[1]
            for which, g in enumerate(groups):
                for index, pair in enumerate(self.groups[g]):
                    found[pair], done = [], 0
                    while done < width:
                        part, inside = divmod(index * width + done, sizes[which])
                        flat = part * sum(sizes) + sum(sizes[:which]) + inside
                        chunk, offset = divmod(flat, piece)
                        size = min(piece - offset, sizes[which] - inside, width - done)
                        found[pair].append((base + chunk, offset, done, size))
                        done += size
            base += self.chunks[1]
        return found

    def update(self, *wanted):
        blocks = self.blocks(1 + len(self.rounds))
        own, other = ([v for i in range(len(self.gathers)) for v in self.gathered[i][core]] for core in range(2))
        instead = {b: self.shares[b][0].updates[self.shares[b][1]] for b in wanted if self.shares.get(b)}
        values = update_blocks(
            blocks, self.places(), own, other, wanted, instead, self.owners, self.columns.last
        )
        self.columns.last = values[:1]
        for b, value in zip(wanted, values):
            if b and b not in self.shares or b in instead:
                returns = [self.returned(b)]
                if b in instead:
                    returns.append(self.shares[b][0].returned(self.shares[b][1]))
                value = shift(value, back(returns), self.fsdp)
            if b in instead:
                wave, block = self.shares[b]
                wave.updates[block] = value
            self.updates[b] = value

    def need(self, b):
        self.columns.last = self.columns.last + [self.updates[b]]

    def returned(self, b):
        return self.owners, self.columns.rounds[self.rounds[b - 1]]

    def found(self, b):
        return self.updates[b], sends(*self.returned(b)) if b else self.owners


def body(iterate, expert_order, fsdp, loop):
    phases, waves, shares, turns = plan(loop, fsdp)
    columns = Columns(iterate, expert_order, phases, fsdp)
    waves = [Wave(columns, *wave, loop) for wave in waves]
    for (wave, block), (other, given) in shares.items():
        waves[wave].shares[block] = waves[other], given
        waves[other].shares[given] = None
    for turn, step, numbers in turns:
        if step == "place":
            found = [waves[wave].found(b) for wave, b in zip(numbers[::2], numbers[1::2])]
            after = [value for value in columns.last if value is not columns.out]
            columns.out = place_slots(columns.out, found, iterate, after)
            columns.last = [columns.out]
        else:
            getattr(columns if step in ("send", "pick") else waves[turn], step)(*numbers)
    return columns.out


def solution(mesh):
    fsdp, loop = mesh.shape["fsdp"], mesh.shape["loop"]
    placed = (P(None, "fsdp", "loop"), P())

    def step(iterate, expert_order):
        return body(iterate, expert_order, fsdp, loop)

    return jax.shard_map(
        step, mesh=mesh, in_specs=placed, out_specs=P(None, "fsdp", "loop"), check_vma=False
    )
```
